32 devices in a mesh: shots: 2 (over y), wide: 16 (over z, x, core).
Axes of the slice: x: 2, y: 2, z: 4, core: 2. Of those that a mesh axis runs over, the one named last changes fastest.
Arguments:
- src_now: float32 [32, 64, 128], P('wide', 'shots'), parts along dimension 1, may hold values from -6 to 6
- src_old: float32 [32, 64, 128], P('wide', 'shots'), parts along dimension 1, may hold values from -6 to 6
- rcv_now: float32 [32, 256, 32], P('wide', 'shots'), parts along dimension 1, may hold values from -6 to 6
- rcv_old: float32 [32, 256, 32], P('wide', 'shots'), parts along dimension 1, may hold values from -6 to 6
- medium: float32 [3, 32, 128, 32], P(None, 'wide'), may hold values from 0.04 to 0.24
- wavelet: float32 [4], replicated, may hold values from -4 to 4
- shot: int32 [6], P('shots'), parts along dimension 0, may hold values from 0 to 31
- traces: float32 [32, 128, 4], P('wide', 'shots'), parts along dimension 1, may hold values from -6 to 6
- rec_x: int32 [32, 128], P('wide', 'shots'), parts along dimension 1, may hold values from 0 to 31
- lag_order: int32 [33], replicated, may hold values from 0 to 32, each once
Outputs:
- src_next: float32 [32, 64, 128], P('wide', 'shots'), parts along dimension 1
- src_prior: float32 [32, 64, 128], P('wide', 'shots'), parts along dimension 1
- rcv_next: float32 [32, 256, 32], P('wide', 'shots'), parts along dimension 1
- rcv_prior: float32 [32, 256, 32], P('wide', 'shots'), parts along dimension 1
- image: float32 [66, 32, 128, 32], P('shots', 'wide'), parts along dimension 0
The draws below stay inside these ranges and needn't reach their ends.
There are 2 independent parts, one for each index of `shots`. The reference program is written for one: setup_inputs(seed, part) draws one part's arguments, and reference() takes and returns one part's arrays. A program takes and returns all parts, laid end to end along the dimension named above; an argument that names none is the same for every part. Nothing has to cross between parts.
Inputs may be any that keep to these rules, and one draw needn't show every extreme that they name: `lag_order`: each of the 33 lag slots once.
All inputs are finite; a program needn't handle non-finite values.
Results may differ from the reference program's by a relative error of at most 0.0003.
Values sent between devices are 32-bit elements; how exact they have to be, the bound alone decides.
No kernel may reach another device: no remote copies, remote signals or barrier semaphores. Data moves between devices by JAX's collectives and lax.ppermute only.
A program may use at most 64 MiB of HBM per device.

```python
import math
import jax
import jax.numpy as jnp
from jax import lax

Z = 128
RX = 64
STEPS = 4
LAGS = 33
X = 32
Y = 32


def place_ends(values, key, smallest, high):
    extent = values.shape
    spot = [jax.random.randint(jax.random.fold_in(key, axis), (), 0, extent[axis]) for axis in range(len(extent))]
    values = values.at[tuple(spot)].set(smallest)
    longest = extent.index(max(extent))
    spot[longest] = (spot[longest] + 1) % extent[longest]
    return values.at[tuple(spot)].set(high)


def shard_levels(own_key, extent, cuts, low, high):
    def one(axis_at, shards_of):
        steps = jax.random.uniform(jax.random.fold_in(jax.random.fold_in(own_key, 6), axis_at), (shards_of,), jnp.float32, low / len(cuts), high / len(cuts))
        return jnp.repeat(jnp.exp(steps), extent[axis_at] // shards_of).reshape((-1,) + (1,) * (len(extent) - axis_at - 1))

    gain = one(*cuts[0])
    for cut in cuts[1:]:
        gain = gain * one(*cut)
    return gain


def normal_values(key, extent, scale, reach, split=(), kind=jnp.bfloat16):
    entries = scale * jax.random.normal(key, extent, jnp.float32)
    if split:
        entries = entries * shard_levels(key, extent, split, -0.22, 0.18)
    return jnp.clip(entries, -reach, reach).astype(kind)


def setup_inputs(seed: int = 0, part: int = 0) -> dict:
    key_of = jax.random.split(jax.random.key(seed), 11)
    part_keys = jax.random.split(jax.random.fold_in(key_of[10], part), 11)
    return {
        "src_now": normal_values(part_keys[0], (X, Y, Z), 1.0, 6.0, ((0, 16),), jnp.float32),
        "src_old": normal_values(part_keys[1], (X, Y, Z), 1.0, 6.0, ((0, 16),), jnp.float32),
        "rcv_now": normal_values(part_keys[2], (Y, Z, X), 1.0, 6.0, ((0, 16),), jnp.float32),
        "rcv_old": normal_values(part_keys[3], (Y, Z, X), 1.0, 6.0, ((0, 16),), jnp.float32),
        "medium": jnp.clip(jnp.exp(math.log(0.24) - 1.7917595 * jax.random.uniform(key_of[4], (3, Y, Z, X), jnp.float32) ** shard_levels(key_of[4], (3, Y, Z, X), ((1, 16),), -0.2, 0.2)), 0.04, 0.24),
        "wavelet": normal_values(key_of[5], (STEPS,), 1.0, 4.0, (), jnp.float32),
        "shot": jax.random.randint(part_keys[6], (3,), 0, min(X, Y, Z)).astype(jnp.int32),
        "traces": normal_values(part_keys[7], (Y, RX, STEPS), 1.0, 6.0, ((0, 16),), jnp.float32),
        "rec_x": place_ends(jax.random.randint(part_keys[8], (Y, RX), 0, X), jax.random.fold_in(part_keys[8], 1), 0, X - 1).astype(jnp.int32),
        "lag_order": jax.random.permutation(key_of[9], LAGS).astype(jnp.int32),
    }


def window_sum(padded, dim, count):
    def window_at(start):
        return lax.slice_in_dim(padded, start, start + count, axis=dim)
    return (-1.0 / 12.0) * (window_at(0) + window_at(4)) + (4.0 / 3.0) * (window_at(1) + window_at(3)) - 2.5 * window_at(2)


def widen(field, dim):
    widths = [(0, 0)] * field.ndim
    widths[dim] = (2, 2)
    return jnp.pad(field, widths)


def second(field, dim):
    return window_sum(widen(field, dim), dim, field.shape[dim])


def lagged(snaps, lag_order):
    half = (lag_order.shape[0] - 1) // 2
    cells_x = snaps[0][0].shape[2]
    widths = ((0, 0), (0, 0), (half, half))
    padded = [(jnp.pad(source, widths), jnp.pad(receiver, widths)) for source, receiver in snaps]

    def one_plane(slot):
        offset = slot.astype(jnp.int32) - half
        total = None
        for source, receiver in padded:
            moved_src = lax.dynamic_slice_in_dim(source, (half - offset).astype(jnp.int32), cells_x, 2)
            moved_rcv = lax.dynamic_slice_in_dim(receiver, (half + offset).astype(jnp.int32), cells_x, 2)
            product = moved_src * moved_rcv
            total = product if total is None else total + product
        return total

    return lax.map(one_plane, lag_order)


def reference(src_now, src_old, rcv_now, rcv_old, medium, wavelet, shot, traces, rec_x, lag_order):
    cells_x, cells_y, cells_z = src_now.shape
    src_speed = jnp.transpose(medium, (0, 3, 1, 2))
    shot_cell = ((jnp.arange(cells_x, dtype=jnp.int32) == shot[0]).astype(jnp.float32)[:, None, None]
                 * (jnp.arange(cells_y, dtype=jnp.int32) == shot[1]).astype(jnp.float32)[None, :, None]
                 * (jnp.arange(cells_z, dtype=jnp.int32) == shot[2]).astype(jnp.float32)[None, None, :])
    onehot = (rec_x[:, :, None] == jnp.arange(cells_x, dtype=jnp.int32)[None, None, :]).astype(jnp.float32)
    snaps = []
    for step in range(wavelet.shape[0]):
        spread = src_speed[0] * second(src_now, 0) + src_speed[1] * second(src_now, 1) + src_speed[2] * second(src_now, 2)
        src_new = 2.0 * src_now - src_old + spread - wavelet[step] * shot_cell
        spread_rcv = medium[0] * second(rcv_now, 2) + medium[1] * second(rcv_now, 0) + medium[2] * second(rcv_now, 1)
        rcv_new = 2.0 * rcv_now - rcv_old + spread_rcv
        surface = jnp.einsum("yr,yrx->yx", traces[:, :, step], onehot, precision=lax.Precision.HIGHEST)
        rcv_new = rcv_new.at[:, 0, :].add(surface)
        src_old, src_now = src_now, src_new
        rcv_old, rcv_now = rcv_now, rcv_new
        if step % 2 == 1:
            snaps.append((jnp.transpose(src_now, (1, 2, 0)), rcv_now))
    image = lagged(snaps, lag_order)
    return src_now, src_old, rcv_now, rcv_old, image
```

```python
import functools

import jax
import jax.numpy as jnp
from jax import lax
from jax.experimental import pallas as pl
from jax.experimental.pallas import tpu as pltpu
from jax.sharding import PartitionSpec as P

SLAB, CHIP, STEPS, EDGE = 2, 4, 4, 8
NEAR, FAR = 4.0 / 3.0, -1.0 / 12.0
CHAINS = 3
RCV, SRC_X, SRC_Y = range(CHAINS)
HALF_NOW = (CHIP + 2 * CHIP) // 2
HALF_OLD = (CHIP + CHIP) // 2
FETCH = 24

VMEM = pl.BlockSpec(memory_space=pltpu.VMEM)
SMEM = pl.BlockSpec(memory_space=pltpu.SMEM)


def call(kernel, operands, outs, scratch, scalars):
    size = sum(4 * o.size for o in operands[scalars:])
    size += sum(4 * functools.reduce(lambda a, b: a * b, s) for s in (*outs, *scratch))
    return pl.pallas_call(
        kernel,
        out_shape=[jax.ShapeDtypeStruct(s, jnp.float32) for s in outs],
        in_specs=[SMEM] * scalars + [VMEM] * (len(operands) - scalars),
        out_specs=[VMEM] * len(outs),
        scratch_shapes=[pltpu.VMEM(s, jnp.float32) for s in scratch],
        compiler_params=pltpu.CompilerParams(vmem_limit_bytes=size + size // 4 + (8 << 20)),
    )(*operands)


def each(count, rows, body):
    if rows <= 32:
        for i in range(count):
            body(i)
    else:
        lax.fori_loop(0, count, lambda i, _: (body(i), 0)[1], 0)


def blocks(rows):
    size = min(rows, 32)
    return [(b, size) for b in range(0, rows, size)]


def pack(src_now, src_old, rcv_now, rcv_old, med, traces, rec_x, send, loc, wide_now, wide_rest):
    rows, depth = src_now.shape[1:]
    steps, cells = traces.shape[1], loc.shape[1]
    for wide in (wide_now, wide_rest):
        count = wide.shape[0]
        wide[:, 0:EDGE, :] = jnp.zeros((count, EDGE, depth), jnp.float32)
        wide[:, EDGE + rows :, :] = jnp.zeros((count, EDGE, depth), jnp.float32)
    for h in range(SLAB):
        wide_now[h, EDGE : EDGE + rows, :] = src_now[h]
        wide_rest[h, EDGE : EDGE + rows, :] = src_old[h]
        for k in range(3):
            wide_rest[SLAB * (k + 1) + h, EDGE : EDGE + rows, :] = med[k, h]
    for j in range(send.shape[0]):
        chip, core = divmod(j, 2)
        now_at = EDGE + CHIP * chip - CHIP + HALF_NOW * core
        old_at = EDGE + CHIP * chip - SLAB + HALF_OLD * core
        for h in range(SLAB):
            base = FETCH * h
            send[j, base : base + HALF_NOW, :] = wide_now[h, now_at : now_at + HALF_NOW, :]
            for k in range(4):
                at = base + HALF_NOW + HALF_OLD * k
                send[j, at : at + HALF_OLD, :] = wide_rest[
                    SLAB * k + h, old_at : old_at + HALF_OLD, :
                ]
    for h in range(SLAB):
        loc[h] = rcv_now[h]
        loc[SLAB + h] = src_now[h]
        loc[2 * SLAB + h] = rcv_old[h]
        loc[3 * SLAB + h] = src_old[h]
        for k in range(3):
            loc[(4 + k) * SLAB + h] = med[k, h]
    lane = lax.broadcasted_iota(jnp.int32, (cells, depth), 1)
    place = lax.broadcasted_iota(jnp.int32, (cells, rec_x.shape[1]), 0)
    surface = jnp.zeros((cells, depth), jnp.float32)
    for h in range(SLAB):
        hit = rec_x[h : h + 1, :] == place
        for s in range(steps):
            column = jnp.sum(jnp.where(hit, traces[h, s : s + 1, :], 0.0), axis=1, keepdims=True)
            surface = jnp.where(lane == steps * h + s, column, surface)
    loc[7 * SLAB] = surface


def advance(now, now_at, old, old_at, med, med_at, new, new_pad, count, pad, rows, across, extra):
    depth = now.shape[2]
    lane = lax.broadcasted_iota(jnp.int32, (8, depth), 1)
    weight = [
        jnp.where(lane >= 1, NEAR, 0.0),
        jnp.where(lane < depth - 1, NEAR, 0.0),
        jnp.where(lane >= 2, FAR, 0.0),
        jnp.where(lane < depth - 2, FAR, 0.0),
    ]

    def one(i):
        w = now_at + i
        for b, size in blocks(rows):
            taps = [jnp.concatenate([t] * (size // 8), axis=0) for t in weight]

            def at(plane, shift):
                return now[plane, pad + b + shift : pad + b + shift + size, :]

            here = at(w, 0)
            centre = -2.5 * here
            plane_sum = (
                centre
                + NEAR * (at(w - 1, 0) + at(w + 1, 0))
                + FAR * (at(w - 2, 0) + at(w + 2, 0))
            )
            row_sum = (
                centre
                + NEAR * (at(w, -1) + at(w, 1))
                + FAR * (at(w, -2) + at(w, 2))
            )
            depth_sum = (
                centre
                + taps[0] * pltpu.roll(here, 1, 1)
                + taps[1] * pltpu.roll(here, depth - 1, 1)
                + taps[2] * pltpu.roll(here, 2, 1)
                + taps[3] * pltpu.roll(here, depth - 2, 1)
            )
            m = [med(k, med_at + i)[b : b + size, :] for k in range(3)]
            value = 2.0 * here - old(old_at + i)[b : b + size, :]
            value = value + m[across] * plane_sum + m[1 - across] * row_sum + m[2] * depth_sum
            if extra is not None:
                value = value + extra(i, b, size)
            new[i, new_pad + b : new_pad + b + size, :] = value

    each(count, rows, one)


def shoot(new, pad, first, count, plane, row, depth_at, amount):
    local = plane - first

    @pl.when((local >= 0) & (local < count))
    def _():
        lane = lax.broadcasted_iota(jnp.int32, (1, new.shape[2]), 1)
        spot = (pl.ds(local, 1), pl.ds(pad + row, 1), slice(None))
        new[spot] = new[spot] + jnp.where(lane == depth_at, -amount, 0.0)[None]


def surface_at(surf, first, step, steps):
    def extra(i, b, size):
        held = surf(first + i // SLAB)[b : b + size, :]
        depth = held.shape[1]
        lane = lax.broadcasted_iota(jnp.int32, (size, depth), 1)
        total = jnp.zeros_like(held)
        shift = (i % SLAB) * steps + step
        if isinstance(shift, int):
            return jnp.where(lane == 0, pltpu.roll(held, (depth - shift) % depth, 1), 0.0)
        for s in range(SLAB):
            moved = pltpu.roll(held, (depth - s * steps - step) % depth, 1)
            total = jnp.where((lane == 0) & (i % SLAB == s), moved, total)
        return total

    return extra


def clear(window, pad, rows):
    count, _, depth = window.shape
    zero = jnp.zeros((count, pad, depth), jnp.float32)
    window[:, 0:pad, :] = zero
    window[:, pad + rows :, :] = zero


def place(window, at, pad, value):
    window[at, pad : pad + value.shape[0], :] = value


def first_half(
    where, shot, wavelet, loc, sib, near, near_sib, got, got_sib, edge, carry,
    now_r, now_x, now_y, old_r, old_x, old_y, med_y, med_x, surf, new_r, new_x, new_y,
):
    rows = loc.shape[1]
    core, right, chip = where[0], where[1], where[2]
    nows, olds, news = (now_r, now_x, now_y), (old_r, old_x, old_y), (new_r, new_x, new_y)
    for window in (*nows, *news):
        clear(window, EDGE, rows)
    window_old = 2 * HALF_OLD
    for src, q in ((loc, core), (sib, 1 - core)):
        for p in range(SLAB):
            place(now_r, CHIP + SLAB * q + p, EDGE, src[p])
            place(now_x, CHIP + SLAB * q + p, EDGE, src[SLAB + p])
            old_r[SLAB + SLAB * q + p] = src[2 * SLAB + p]
            old_x[SLAB + SLAB * q + p] = src[3 * SLAB + p]
            for k in range(3):
                med_y[window_old * k + SLAB + SLAB * q + p] = src[(4 + k) * SLAB + p]
        surf[1 + q] = src[7 * SLAB]
    for src, side in ((near, right), (near_sib, 1 - right)):
        for p in range(SLAB):
            for low in range(2):
                at = 2 * CHIP * side + SLAB * low + p
                place(now_r, at, EDGE, src[2 * SLAB * low + p])
                place(now_x, at, EDGE, src[2 * SLAB * low + SLAB + p])
            at = (SLAB + CHIP) * side + p
            old_r[at] = src[4 * SLAB + p]
            old_x[at] = src[5 * SLAB + p]
            for k in range(3):
                med_y[window_old * k + at] = src[(6 + k) * SLAB + p]
        surf[3 * side] = src[9 * SLAB]
    for src, q in ((got, core), (got_sib, 1 - core)):
        for p in range(HALF_NOW):
            place(now_y, HALF_NOW * q + p, EDGE, src[pl.ds(p, rows, stride=FETCH), :])
        for p in range(HALF_OLD):
            old_y[HALF_OLD * q + p] = src[pl.ds(HALF_NOW + p, rows, stride=FETCH), :]
            for k in range(3):
                med_x[window_old * k + HALF_OLD * q + p] = src[
                    pl.ds(HALF_NOW + HALF_OLD * (k + 1) + p, rows, stride=FETCH), :
                ]

    def medium_of(ref):
        return lambda k, i: ref[window_old * k + i]

    first = CHIP * chip - SLAB
    media = (med_y, med_x, med_y)
    spot = (None, (shot[0], shot[1]), (shot[1], shot[0]))
    for c in range(CHAINS):
        across = 0 if c == SRC_X else 1
        advance(
            nows[c], SLAB, lambda i: olds[c][i], 0, medium_of(media[c]), 0, news[c], EDGE,
            window_old, EDGE, rows, across,
            surface_at(lambda i: surf[i], 0, 0, STEPS) if c == RCV else None,
        )
        if c != RCV:
            shoot(news[c], EDGE, first, window_old, *spot[c], shot[2], wavelet[0])
        advance(
            news[c], SLAB, lambda i: nows[c][CHIP + i, EDGE : EDGE + rows, :], 0,
            medium_of(media[c]), SLAB, edge.at[c], 0, CHIP, EDGE, rows, across,
            surface_at(lambda i: surf[i], 1, 1, STEPS) if c == RCV else None,
        )
        if c != RCV:
            shoot(edge.at[c], 0, first + SLAB, CHIP, *spot[c], shot[2], wavelet[1])
    span = SLAB + 2 * SLAB
    for i in range(span):
        at = SLAB * core + i
        for c in range(CHAINS):
            carry[span * c + i] = news[c][at, EDGE : EDGE + rows, :]
        for k in range(3):
            carry[span * (CHAINS + k) + i] = med_y[window_old * k + at]
            carry[span * (CHAINS + 3 + k) + i] = med_x[window_old * k + at]
    for i in range(3):
        carry[span * (CHAINS + 6) + i] = surf[core + i]


def second_half(
    where, shot, wavelet, lag_order, edge, near, near_sib, carry,
    src_next, src_prior, rcv_next, rcv_prior, image,
    now_r, now_x, now_y, new_r, new_x, new_y, end_r, end_x, end_y, slot_of,
):
    rows, depth = carry.shape[1:]
    lags = lag_order.shape[0]
    half = (lags - 1) // 2
    pad = (now_r.shape[1] - rows) // 2
    core, right, chip = where[0], where[1], where[2]
    nows, news, ends = (now_r, now_x, now_y), (new_r, new_x, new_y), (end_r, end_x, end_y)
    for window in (*nows, *news, *ends):
        clear(window, pad, rows)

    def note(k, _):
        slot_of[lag_order[k]] = k
        return 0

    lax.fori_loop(0, lags, note, 0)
    for c in range(CHAINS):
        for p in range(CHIP):
            place(nows[c], CHIP + p, pad, edge[c, p])
            place(nows[c], 2 * CHIP * right + p, pad, near[c, p])
            place(nows[c], 2 * CHIP * (1 - right) + p, pad, near_sib[c, p])
    span = SLAB + 2 * SLAB
    first = CHIP * chip + SLAB * core - SLAB
    spot = (None, (shot[0], shot[1]), (shot[1], shot[0]))
    at_surf = span * (CHAINS + 6)
    for c in (RCV, SRC_Y, SRC_X):
        across = 0 if c == SRC_X else 1
        base = span * (CHAINS + (3 if c == SRC_X else 0))

        def med(k, i):
            return carry[base + span * k + i]

        advance(
            nows[c], SLAB * core + SLAB, lambda i: carry[span * c + i], 0, med, 0, news[c], pad,
            span, pad, rows, across,
            surface_at(lambda i: carry[at_surf + i], 0, 2, STEPS) if c == RCV else None,
        )
        if c != RCV:
            shoot(news[c], pad, first, span, *spot[c], shot[2], wavelet[2])
        advance(
            news[c], SLAB, lambda i: nows[c][CHIP + SLAB * core + i, pad : pad + rows, :], 0,
            med, SLAB, ends[c], pad, SLAB, pad, rows, across,
            surface_at(lambda i: carry[at_surf + i], 1, 3, STEPS) if c == RCV else None,
        )
        if c != RCV:
            shoot(ends[c], pad, first + SLAB, SLAB, *spot[c], shot[2], wavelet[3])
    for p in range(SLAB):
        src_next[p] = end_x[p, pad : pad + rows, :]
        src_prior[p] = new_x[SLAB + p, pad : pad + rows, :]
        rcv_next[p] = end_r[p, pad : pad + rows, :]
        rcv_prior[p] = new_r[SLAB + p, pad : pad + rows, :]
    own = CHIP + SLAB * core
    for slot in range(lags):
        lag = slot - half
        k = slot_of[slot]

        def one(p):
            for b in range(0, rows, 8):
                if b + 8 <= abs(lag) or b >= rows - abs(lag):
                    image[k, p, b : b + 8, :] = jnp.zeros((8, depth), jnp.float32)
                    continue
                back, ahead = pad + b - lag, pad + b + lag
                image[k, p, b : b + 8, :] = (
                    now_y[own + p, back : back + 8, :] * now_r[own + p, ahead : ahead + 8, :]
                    + end_y[p, back : back + 8, :] * end_r[p, ahead : ahead + 8, :]
                )

        for p in range(SLAB):
            one(p)


def on_device(src_now, src_old, rcv_now, rcv_old, medium, wavelet, shot, traces, rec_x, lag_order):
    devices = lax.axis_size("wide")
    chips = devices // 2
    slab, rows, depth = src_now.shape
    assert slab == SLAB and rcv_now.shape == (SLAB, depth, rows) and wavelet.shape[0] == STEPS
    assert rows % 8 == 0 and rows == SLAB * devices
    lags = lag_order.shape[0]
    half = (lags - 1) // 2
    device = lax.axis_index("wide")
    chip, core = device // 2, device % 2
    right = (core == chip % 2).astype(jnp.int32)
    where = jnp.stack([core, right, chip]).astype(jnp.int32)
    swap = [(i, i ^ 1) for i in range(devices)]
    ties = [(2 * c + c % 2, 2 * c + 2 + c % 2) for c in range(chips - 1)]
    ties = ties + [(b, a) for a, b in ties]

    def turned(x):
        return jnp.swapaxes(x, -1, -2)

    rcv_now, rcv_old, medium, traces = map(turned, (rcv_now, rcv_old, medium, traces))
    send, loc = call(
        pack,
        (src_now, src_old, rcv_now, rcv_old, medium, traces, rec_x),
        [(devices, SLAB * FETCH, depth), (7 * SLAB + 1, rows, depth)],
        [(SLAB, rows + 2 * EDGE, depth), (4 * SLAB, rows + 2 * EDGE, depth)],
        0,
    )
    got = lax.all_to_all(send, "wide", 0, 0, tiled=True)
    sib = lax.ppermute(loc, "wide", swap)
    low, high = jnp.where(core == 0, loc, sib), jnp.where(core == 0, sib, loc)
    rim = jnp.where(right == 1, high[2 * SLAB :], low[2 * SLAB :])
    near = lax.ppermute(jnp.concatenate([low[: 2 * SLAB], high[: 2 * SLAB], rim]), "wide", ties)
    near_sib = lax.ppermute(near, "wide", swap)
    got = got.reshape(devices * SLAB * FETCH, depth)
    got_sib = lax.ppermute(got, "wide", swap)

    window, narrow, span = 3 * CHIP, 2 * CHIP, 3 * SLAB
    wide_rows = rows + 2 * EDGE
    edge, carry = call(
        first_half,
        (where, shot, wavelet, loc, sib, near, near_sib, got, got_sib),
        [(CHAINS, CHIP, rows, depth), (span * (CHAINS + 6) + 3, rows, depth)],
        [(window, wide_rows, depth)] * 3
        + [(narrow, rows, depth)] * 3
        + [(3 * narrow, rows, depth)] * 2
        + [(4, rows, depth)]
        + [(narrow, wide_rows, depth)] * 3,
        3,
    )
    near = lax.ppermute(edge, "wide", ties)
    near_sib = lax.ppermute(near, "wide", swap)

    pad = -(-max(half, 2) // 8) * 8
    wide_rows = rows + 2 * pad
    field = (SLAB, rows, depth)
    operands = (where, shot, wavelet, lag_order, edge, near, near_sib, carry)
    outs = [field] * 4 + [(lags, SLAB, rows, depth)]
    scratch = [(window, wide_rows, depth)] * 3 + [(span, wide_rows, depth)] * 3 + [field[:1] + (wide_rows, depth)] * 3
    size = sum(4 * o.size for o in operands[4:])
    size += sum(4 * functools.reduce(lambda a, b: a * b, s) for s in (*outs, *scratch))
    src_next, src_prior, rcv_next, rcv_prior, image = pl.pallas_call(
        second_half,
        out_shape=[jax.ShapeDtypeStruct(s, jnp.float32) for s in outs],
        in_specs=[SMEM] * 4 + [VMEM] * 4,
        out_specs=[VMEM] * 5,
        scratch_shapes=[pltpu.VMEM(s, jnp.float32) for s in scratch] + [pltpu.SMEM((lags,), jnp.int32)],
        compiler_params=pltpu.CompilerParams(vmem_limit_bytes=size + size // 4 + (8 << 20)),
    )(*operands)
    return src_next, src_prior, turned(rcv_next), turned(rcv_prior), turned(image)


def solution(mesh):
    return jax.shard_map(
        on_device,
        mesh=mesh,
        in_specs=(
            P("wide", "shots", None),
            P("wide", "shots", None),
            P("wide", "shots", None),
            P("wide", "shots", None),
            P(None, "wide", None, None),
            P(),
            P("shots"),
            P("wide", "shots", None),
            P("wide", "shots"),
            P(),
        ),
        out_specs=(
            P("wide", "shots", None),
            P("wide", "shots", None),
            P("wide", "shots", None),
            P("wide", "shots", None),
            P("shots", "wide", None, None),
        ),
        check_vma=False,
    )
```

```python
import functools

import jax
import jax.numpy as jnp
from jax import lax
from jax.experimental import pallas as pl
from jax.experimental.pallas import tpu as pltpu
from jax.sharding import PartitionSpec as P

SLAB, CHIP, STEPS, EDGE = 2, 4, 4, 8
NEAR, FAR = 4.0 / 3.0, -1.0 / 12.0
CHAINS = 3
RCV, SRC_X, SRC_Y = range(CHAINS)
HALF_NOW = (CHIP + 2 * CHIP) // 2
HALF_OLD = (CHIP + CHIP) // 2
FETCH = 24

VMEM = pl.BlockSpec(memory_space=pltpu.VMEM)
SMEM = pl.BlockSpec(memory_space=pltpu.SMEM)
HBM = pl.BlockSpec(memory_space=pltpu.HBM)


def call(kernel, operands, outs, scratch, scalars, held=(), far_in=False, far_out=()):
    size = sum(4 * o.size for o in operands[scalars:])
    size += sum(4 * functools.reduce(lambda a, b: a * b, s) for s in (*outs, *scratch))
    if far_in:
        operands = [pltpu.with_memory_space_constraint(o, pltpu.HBM) for o in operands]
    return pl.pallas_call(
        kernel,
        out_shape=[jax.ShapeDtypeStruct(s, jnp.float32) for s in outs],
        in_specs=[SMEM] * scalars + [HBM if far_in else VMEM] * (len(operands) - scalars),
        out_specs=[HBM if n in far_out else VMEM for n in range(len(outs))],
        scratch_shapes=[pltpu.VMEM(s, jnp.float32) for s in scratch] + list(held),
        compiler_params=pltpu.CompilerParams(vmem_limit_bytes=size + size // 4 + (8 << 20)),
    )(*operands)


def each(count, rows, body):
    if rows <= 32:
        for i in range(count):
            body(i)
    else:
        lax.fori_loop(0, count, lambda i, _: (body(i), 0)[1], 0)


def blocks(rows):
    size = min(rows, 32)
    return [(b, size) for b in range(0, rows, size)]


def pack(
    src_now, src_old, rcv_now, rcv_old, med, traces, rec_x, send, loc,
    wide_now, wide_rest, traces_in, rec_in, sems,
):
    rows, depth = src_now.shape[1:]
    steps, cells = traces.shape[1], loc.shape[1]
    inner = pl.ds(EDGE, rows)
    pairs = [(traces, traces_in), (rec_x, rec_in)]
    pairs += [(src_now, wide_now.at[:, inner]), (src_old, wide_rest.at[pl.ds(0, SLAB), inner])]
    pairs += [(med.at[k], wide_rest.at[pl.ds(SLAB * (k + 1), SLAB), inner]) for k in range(3)]
    for n, own in enumerate((rcv_now, src_now, rcv_old, src_old)):
        pairs.append((own, loc.at[pl.ds(n * SLAB, SLAB)]))
    pairs += [(med.at[k], loc.at[pl.ds((4 + k) * SLAB, SLAB)]) for k in range(3)]
    copies = [pltpu.make_async_copy(a, b, sems.at[n]) for n, (a, b) in enumerate(pairs)]
    for copy in copies:
        copy.start()
    for wide in (wide_now, wide_rest):
        count = wide.shape[0]
        wide[:, 0:EDGE, :] = jnp.zeros((count, EDGE, depth), jnp.float32)
        wide[:, EDGE + rows :, :] = jnp.zeros((count, EDGE, depth), jnp.float32)
    for copy in copies[:2]:
        copy.wait()
    lane = lax.broadcasted_iota(jnp.int32, (cells, depth), 1)
    place = lax.broadcasted_iota(jnp.int32, (cells, rec_x.shape[1]), 0)
    surface = jnp.zeros((cells, depth), jnp.float32)
    for h in range(SLAB):
        hit = rec_in[h : h + 1, :] == place
        for s in range(steps):
            column = jnp.sum(jnp.where(hit, traces_in[h, s : s + 1, :], 0.0), axis=1, keepdims=True)
            surface = jnp.where(lane == steps * h + s, column, surface)
    loc[7 * SLAB] = surface
    for copy in copies[2:]:
        copy.wait()
    for j in range(send.shape[0]):
        chip, core = divmod(j, 2)
        now_at = EDGE + CHIP * chip - CHIP + HALF_NOW * core
        old_at = EDGE + CHIP * chip - SLAB + HALF_OLD * core
        for h in range(SLAB):
            base = FETCH * h
            send[j, base : base + HALF_NOW, :] = wide_now[h, now_at : now_at + HALF_NOW, :]
            for k in range(4):
                at = base + HALF_NOW + HALF_OLD * k
                send[j, at : at + HALF_OLD, :] = wide_rest[
                    SLAB * k + h, old_at : old_at + HALF_OLD, :
                ]


def advance(now, now_at, old, old_at, med, med_at, new, new_pad, count, pad, rows, across, extra):
    depth = now.shape[2]
    lane = lax.broadcasted_iota(jnp.int32, (8, depth), 1)
    weight = [
        jnp.where(lane >= 1, NEAR, 0.0),
        jnp.where(lane < depth - 1, NEAR, 0.0),
        jnp.where(lane >= 2, FAR, 0.0),
        jnp.where(lane < depth - 2, FAR, 0.0),
    ]

    def one(i):
        w = now_at + i
        for b, size in blocks(rows):
            taps = [jnp.concatenate([t] * (size // 8), axis=0) for t in weight]

            def at(plane, shift):
                return now[plane, pad + b + shift : pad + b + shift + size, :]

            here = at(w, 0)
            centre = -2.5 * here
            plane_sum = (
                centre
                + NEAR * (at(w - 1, 0) + at(w + 1, 0))
                + FAR * (at(w - 2, 0) + at(w + 2, 0))
            )
            row_sum = (
                centre
                + NEAR * (at(w, -1) + at(w, 1))
                + FAR * (at(w, -2) + at(w, 2))
            )
            depth_sum = (
                centre
                + taps[0] * pltpu.roll(here, 1, 1)
                + taps[1] * pltpu.roll(here, depth - 1, 1)
                + taps[2] * pltpu.roll(here, 2, 1)
                + taps[3] * pltpu.roll(here, depth - 2, 1)
            )
            m = [med(k, med_at + i)[b : b + size, :] for k in range(3)]
            value = 2.0 * here - old(old_at + i)[b : b + size, :]
            value = value + m[across] * plane_sum + m[1 - across] * row_sum + m[2] * depth_sum
            if extra is not None:
                value = value + extra(i, b, size)
            new[i, new_pad + b : new_pad + b + size, :] = value

    each(count, rows, one)


def shoot(new, pad, first, count, plane, row, depth_at, amount):
    local = plane - first

    @pl.when((local >= 0) & (local < count))
    def _():
        lane = lax.broadcasted_iota(jnp.int32, (1, new.shape[2]), 1)
        spot = (pl.ds(local, 1), pl.ds(pad + row, 1), slice(None))
        new[spot] = new[spot] + jnp.where(lane == depth_at, -amount, 0.0)[None]


def surface_at(surf, first, step, steps):
    def extra(i, b, size):
        held = surf(first + i // SLAB)[b : b + size, :]
        depth = held.shape[1]
        lane = lax.broadcasted_iota(jnp.int32, (size, depth), 1)
        total = jnp.zeros_like(held)
        shift = (i % SLAB) * steps + step
        if isinstance(shift, int):
            return jnp.where(lane == 0, pltpu.roll(held, (depth - shift) % depth, 1), 0.0)
        for s in range(SLAB):
            moved = pltpu.roll(held, (depth - s * steps - step) % depth, 1)
            total = jnp.where((lane == 0) & (i % SLAB == s), moved, total)
        return total

    return extra


def clear(window, pad, rows):
    count, _, depth = window.shape
    zero = jnp.zeros((count, pad, depth), jnp.float32)
    window[:, 0:pad, :] = zero
    window[:, pad + rows :, :] = zero


def place(window, at, pad, value):
    window[at, pad : pad + value.shape[0], :] = value


def first_half(
    where, shot, wavelet, loc, sib, near, near_sib, got, got_sib, edge, carry,
    now_r, now_x, now_y, old_r, old_x, old_y, med_y, med_x, surf, new_r, new_x, new_y,
):
    rows = loc.shape[1]
    core, right, chip = where[0], where[1], where[2]
    nows, olds, news = (now_r, now_x, now_y), (old_r, old_x, old_y), (new_r, new_x, new_y)
    for window in (*nows, *news):
        clear(window, EDGE, rows)
    window_old = 2 * HALF_OLD
    for src, q in ((loc, core), (sib, 1 - core)):
        for p in range(SLAB):
            place(now_r, CHIP + SLAB * q + p, EDGE, src[p])
            place(now_x, CHIP + SLAB * q + p, EDGE, src[SLAB + p])
            old_r[SLAB + SLAB * q + p] = src[2 * SLAB + p]
            old_x[SLAB + SLAB * q + p] = src[3 * SLAB + p]
            for k in range(3):
                med_y[window_old * k + SLAB + SLAB * q + p] = src[(4 + k) * SLAB + p]
        surf[1 + q] = src[7 * SLAB]
    for src, side in ((near, right), (near_sib, 1 - right)):
        for p in range(SLAB):
            for low in range(2):
                at = 2 * CHIP * side + SLAB * low + p
                place(now_r, at, EDGE, src[2 * SLAB * low + p])
                place(now_x, at, EDGE, src[2 * SLAB * low + SLAB + p])
            at = (SLAB + CHIP) * side + p
            old_r[at] = src[4 * SLAB + p]
            old_x[at] = src[5 * SLAB + p]
            for k in range(3):
                med_y[window_old * k + at] = src[(6 + k) * SLAB + p]
        surf[3 * side] = src[9 * SLAB]
    for src, q in ((got, core), (got_sib, 1 - core)):
        for p in range(HALF_NOW):
            place(now_y, HALF_NOW * q + p, EDGE, src[pl.ds(p, rows, stride=FETCH), :])
        for p in range(HALF_OLD):
            old_y[HALF_OLD * q + p] = src[pl.ds(HALF_NOW + p, rows, stride=FETCH), :]
            for k in range(3):
                med_x[window_old * k + HALF_OLD * q + p] = src[
                    pl.ds(HALF_NOW + HALF_OLD * (k + 1) + p, rows, stride=FETCH), :
                ]

    def medium_of(ref):
        return lambda k, i: ref[window_old * k + i]

    first = CHIP * chip - SLAB
    media = (med_y, med_x, med_y)
    spot = (None, (shot[0], shot[1]), (shot[1], shot[0]))
    for c in range(CHAINS):
        across = 0 if c == SRC_X else 1
        advance(
            nows[c], SLAB, lambda i: olds[c][i], 0, medium_of(media[c]), 0, news[c], EDGE,
            window_old, EDGE, rows, across,
            surface_at(lambda i: surf[i], 0, 0, STEPS) if c == RCV else None,
        )
        if c != RCV:
            shoot(news[c], EDGE, first, window_old, *spot[c], shot[2], wavelet[0])
        advance(
            news[c], SLAB, lambda i: nows[c][CHIP + i, EDGE : EDGE + rows, :], 0,
            medium_of(media[c]), SLAB, edge.at[c], 0, CHIP, EDGE, rows, across,
            surface_at(lambda i: surf[i], 1, 1, STEPS) if c == RCV else None,
        )
        if c != RCV:
            shoot(edge.at[c], 0, first + SLAB, CHIP, *spot[c], shot[2], wavelet[1])
    span = SLAB + 2 * SLAB
    for i in range(span):
        at = SLAB * core + i
        for c in range(CHAINS):
            carry[span * c + i] = news[c][at, EDGE : EDGE + rows, :]
        for k in range(3):
            carry[span * (CHAINS + k) + i] = med_y[window_old * k + at]
            carry[span * (CHAINS + 3 + k) + i] = med_x[window_old * k + at]
    for i in range(3):
        carry[span * (CHAINS + 6) + i] = surf[core + i]


def second_half(
    where, shot, wavelet, lag_order, edge, near, near_sib, carry,
    src_next, src_prior, rcv_next, rcv_prior, image,
    now_r, now_x, now_y, new_r, new_x, new_y, end_r, end_x, end_y, planes, slot_of, sems,
):
    rows, depth = carry.shape[1:]
    lags = lag_order.shape[0]
    half = (lags - 1) // 2
    pad = (now_r.shape[1] - rows) // 2
    core, right, chip = where[0], where[1], where[2]
    nows, news, ends = (now_r, now_x, now_y), (new_r, new_x, new_y), (end_r, end_x, end_y)
    for window in (*nows, *news, *ends):
        clear(window, pad, rows)

    def note(k, _):
        slot_of[lag_order[k]] = k
        return 0

    lax.fori_loop(0, lags, note, 0)
    for c in range(CHAINS):
        for p in range(CHIP):
            place(nows[c], CHIP + p, pad, edge[c, p])
            place(nows[c], 2 * CHIP * right + p, pad, near[c, p])
            place(nows[c], 2 * CHIP * (1 - right) + p, pad, near_sib[c, p])
    span = SLAB + 2 * SLAB
    first = CHIP * chip + SLAB * core - SLAB
    spot = (None, (shot[0], shot[1]), (shot[1], shot[0]))
    at_surf = span * (CHAINS + 6)
    for c in (RCV, SRC_Y, SRC_X):
        across = 0 if c == SRC_X else 1
        base = span * (CHAINS + (3 if c == SRC_X else 0))

        def med(k, i):
            return carry[base + span * k + i]

        advance(
            nows[c], SLAB * core + SLAB, lambda i: carry[span * c + i], 0, med, 0, news[c], pad,
            span, pad, rows, across,
            surface_at(lambda i: carry[at_surf + i], 0, 2, STEPS) if c == RCV else None,
        )
        if c != RCV:
            shoot(news[c], pad, first, span, *spot[c], shot[2], wavelet[2])
        advance(
            news[c], SLAB, lambda i: nows[c][CHIP + SLAB * core + i, pad : pad + rows, :], 0,
            med, SLAB, ends[c], pad, SLAB, pad, rows, across,
            surface_at(lambda i: carry[at_surf + i], 1, 3, STEPS) if c == RCV else None,
        )
        if c != RCV:
            shoot(ends[c], pad, first + SLAB, SLAB, *spot[c], shot[2], wavelet[3])
    for p in range(SLAB):
        src_next[p] = end_x[p, pad : pad + rows, :]
        src_prior[p] = new_x[SLAB + p, pad : pad + rows, :]
        rcv_next[p] = end_r[p, pad : pad + rows, :]
        rcv_prior[p] = new_r[SLAB + p, pad : pad + rows, :]
    own = CHIP + SLAB * core
    copies = []
    for slot in range(lags):
        lag = slot - half
        for p in range(SLAB):
            for b in range(0, rows, 8):
                if b + 8 <= abs(lag) or b >= rows - abs(lag):
                    planes[slot, p, b : b + 8, :] = jnp.zeros((8, depth), jnp.float32)
                    continue
                back, ahead = pad + b - lag, pad + b + lag
                planes[slot, p, b : b + 8, :] = (
                    now_y[own + p, back : back + 8, :] * now_r[own + p, ahead : ahead + 8, :]
                    + end_y[p, back : back + 8, :] * end_r[p, ahead : ahead + 8, :]
                )
        copies.append(
            pltpu.make_async_copy(planes.at[slot], image.at[slot_of[slot]], sems.at[slot])
        )
        copies[-1].start()
    for copy in copies:
        copy.wait()


def on_device(src_now, src_old, rcv_now, rcv_old, medium, wavelet, shot, traces, rec_x, lag_order):
    devices = lax.axis_size("wide")
    chips = devices // 2
    slab, rows, depth = src_now.shape
    assert slab == SLAB and rcv_now.shape == (SLAB, depth, rows) and wavelet.shape[0] == STEPS
    assert rows % 8 == 0 and rows == SLAB * devices
    lags = lag_order.shape[0]
    half = (lags - 1) // 2
    device = lax.axis_index("wide")
    chip, core = device // 2, device % 2
    right = (core == chip % 2).astype(jnp.int32)
    where = jnp.stack([core, right, chip]).astype(jnp.int32)
    swap = [(i, i ^ 1) for i in range(devices)]
    ties = [(2 * c + c % 2, 2 * c + 2 + c % 2) for c in range(chips - 1)]
    ties = ties + [(b, a) for a, b in ties]

    def turned(x):
        return jnp.swapaxes(x, -1, -2)

    rcv_now, rcv_old, medium, traces = map(turned, (rcv_now, rcv_old, medium, traces))
    send, loc = call(
        pack,
        (src_now, src_old, rcv_now, rcv_old, medium, traces, rec_x),
        [(devices, SLAB * FETCH, depth), (7 * SLAB + 1, rows, depth)],
        [(SLAB, rows + 2 * EDGE, depth), (4 * SLAB, rows + 2 * EDGE, depth), traces.shape],
        0,
        [pltpu.VMEM(rec_x.shape, jnp.int32), pltpu.SemaphoreType.DMA((14,))],
        far_in=True,
    )
    got = lax.all_to_all(send, "wide", 0, 0, tiled=True)
    sib = lax.ppermute(loc, "wide", swap)
    low, high = jnp.where(core == 0, loc, sib), jnp.where(core == 0, sib, loc)
    rim = jnp.where(right == 1, high[2 * SLAB :], low[2 * SLAB :])
    near = lax.ppermute(jnp.concatenate([low[: 2 * SLAB], high[: 2 * SLAB], rim]), "wide", ties)
    near_sib = lax.ppermute(near, "wide", swap)
    got = got.reshape(devices * SLAB * FETCH, depth)
    got_sib = lax.ppermute(got, "wide", swap)

    window, narrow, span = 3 * CHIP, 2 * CHIP, 3 * SLAB
    wide_rows = rows + 2 * EDGE
    edge, carry = call(
        first_half,
        (where, shot, wavelet, loc, sib, near, near_sib, got, got_sib),
        [(CHAINS, CHIP, rows, depth), (span * (CHAINS + 6) + 3, rows, depth)],
        [(window, wide_rows, depth)] * 3
        + [(narrow, rows, depth)] * 3
        + [(3 * narrow, rows, depth)] * 2
        + [(4, rows, depth)]
        + [(narrow, wide_rows, depth)] * 3,
        3,
    )
    near = lax.ppermute(edge, "wide", ties)
    near_sib = lax.ppermute(near, "wide", swap)

    pad = -(-max(half, 2) // 8) * 8
    wide_rows = rows + 2 * pad
    field = (SLAB, rows, depth)
    src_next, src_prior, rcv_next, rcv_prior, image = call(
        second_half,
        (where, shot, wavelet, lag_order, edge, near, near_sib, carry),
        [field] * 4 + [(lags, SLAB, rows, depth)],
        [(window, wide_rows, depth)] * 3
        + [(span, wide_rows, depth)] * 3
        + [(SLAB, wide_rows, depth)] * 3
        + [(lags, SLAB, rows, depth)],
        4,
        [pltpu.SMEM((lags,), jnp.int32), pltpu.SemaphoreType.DMA((lags,))],
        far_out=(4,),
    )
    return src_next, src_prior, turned(rcv_next), turned(rcv_prior), turned(image)


def solution(mesh):
    return jax.shard_map(
        on_device,
        mesh=mesh,
        in_specs=(
            P("wide", "shots", None),
            P("wide", "shots", None),
            P("wide", "shots", None),
            P("wide", "shots", None),
            P(None, "wide", None, None),
            P(),
            P("shots"),
            P("wide", "shots", None),
            P("wide", "shots"),
            P(),
        ),
        out_specs=(
            P("wide", "shots", None),
            P("wide", "shots", None),
            P("wide", "shots", None),
            P("wide", "shots", None),
            P("shots", "wide", None, None),
        ),
        check_vma=False,
    )
```

```python
import functools

import jax
import jax.numpy as jnp
from jax import lax
from jax.experimental import pallas as pl
from jax.experimental.pallas import tpu as pltpu
from jax.sharding import PartitionSpec as P

SLAB, CHIP, STEPS, EDGE = 2, 4, 4, 8
NEAR, FAR = 4.0 / 3.0, -1.0 / 12.0
RCV, SRC = 0, 1
SPAN = 3 * SLAB
HALF_NOW = (CHIP + 2 * CHIP) // 2
HALF_OLD = (CHIP + CHIP) // 2
FETCH = 24

VMEM = pl.BlockSpec(memory_space=pltpu.VMEM)
SMEM = pl.BlockSpec(memory_space=pltpu.SMEM)
HBM = pl.BlockSpec(memory_space=pltpu.HBM)


def call(kernel, operands, outs, scratch, scalars, held=(), far_in=False, far_out=()):
    size = sum(4 * o.size for o in operands[scalars:])
    size += sum(4 * functools.reduce(lambda a, b: a * b, s) for s in (*outs, *scratch))
    if far_in:
        operands = [pltpu.with_memory_space_constraint(o, pltpu.HBM) for o in operands]
    return pl.pallas_call(
        kernel,
        out_shape=[jax.ShapeDtypeStruct(s, jnp.float32) for s in outs],
        in_specs=[SMEM] * scalars + [HBM if far_in else VMEM] * (len(operands) - scalars),
        out_specs=[HBM if n in far_out else VMEM for n in range(len(outs))],
        scratch_shapes=[pltpu.VMEM(s, jnp.float32) for s in scratch] + list(held),
        compiler_params=pltpu.CompilerParams(vmem_limit_bytes=size + size // 4 + (8 << 20)),
    )(*operands)


def each(count, rows, body):
    if rows <= 32:
        for i in range(count):
            body(i)
    else:
        lax.fori_loop(0, count, lambda i, _: (body(i), 0)[1], 0)


def blocks(rows):
    size = min(rows, 32)
    return [(b, size) for b in range(0, rows, size)]


def gather(
    src_now, src_old, rcv_now, rcv_old, med, traces, rec_x, wide, loc, traces_in, rec_in, sems
):
    rows, depth = src_now.shape[1:]
    steps, cells = traces.shape[1], loc.shape[1]
    inner = pl.ds(EDGE, rows)
    pairs = [(traces, traces_in), (rec_x, rec_in)]
    for n, own in enumerate((rcv_now, src_now, rcv_old, src_old)):
        pairs.append((own, loc.at[pl.ds(n * SLAB, SLAB)]))
    pairs += [(med.at[k], loc.at[pl.ds((4 + k) * SLAB, SLAB)]) for k in range(3)]
    for n, own in enumerate((src_now, src_old, med.at[0], med.at[1], med.at[2])):
        pairs.append((own, wide.at[pl.ds(n * SLAB, SLAB), inner]))
    copies = [pltpu.make_async_copy(a, b, sems.at[n]) for n, (a, b) in enumerate(pairs)]
    for copy in copies:
        copy.start()
    clear(wide, EDGE, rows)
    for copy in copies[:2]:
        copy.wait()
    lane = lax.broadcasted_iota(jnp.int32, (cells, depth), 1)
    place = lax.broadcasted_iota(jnp.int32, (cells, rec_x.shape[1]), 0)
    surface = jnp.zeros((cells, depth), jnp.float32)
    for h in range(SLAB):
        hit = rec_in[h : h + 1, :] == place
        for s in range(steps):
            column = jnp.sum(jnp.where(hit, traces_in[h, s : s + 1, :], 0.0), axis=1, keepdims=True)
            surface = jnp.where(lane == steps * h + s, column, surface)
    loc[7 * SLAB] = surface
    for copy in copies[2:]:
        copy.wait()


def pack(wide, send):
    for j in range(send.shape[0]):
        chip, core = divmod(j, 2)
        now_at = EDGE + CHIP * chip - CHIP + HALF_NOW * core
        old_at = EDGE + CHIP * chip - SLAB + HALF_OLD * core
        for h in range(SLAB):
            at = FETCH * h
            send[j, at : at + HALF_NOW, :] = wide[h, now_at : now_at + HALF_NOW, :]
            for k in range(4):
                at = FETCH * h + HALF_NOW + HALF_OLD * k
                plane = SLAB * (k + 1) + h
                send[j, at : at + HALF_OLD, :] = wide[plane, old_at : old_at + HALF_OLD, :]


def advance(now, now_at, old, old_at, med, med_at, new, new_pad, count, pad, rows, across, extra):
    depth = now.shape[2]
    lane = lax.broadcasted_iota(jnp.int32, (8, depth), 1)
    weight = [
        jnp.where(lane >= 1, NEAR, 0.0),
        jnp.where(lane < depth - 1, NEAR, 0.0),
        jnp.where(lane >= 2, FAR, 0.0),
        jnp.where(lane < depth - 2, FAR, 0.0),
    ]

    def one(i):
        w = now_at + i
        for b, size in blocks(rows):
            taps = [jnp.concatenate([t] * (size // 8), axis=0) for t in weight]

            def at(plane, shift):
                return now[plane, pad + b + shift : pad + b + shift + size, :]

            here = at(w, 0)
            centre = -2.5 * here
            plane_sum = (
                centre
                + NEAR * (at(w - 1, 0) + at(w + 1, 0))
                + FAR * (at(w - 2, 0) + at(w + 2, 0))
            )
            row_sum = (
                centre
                + NEAR * (at(w, -1) + at(w, 1))
                + FAR * (at(w, -2) + at(w, 2))
            )
            depth_sum = (
                centre
                + taps[0] * pltpu.roll(here, 1, 1)
                + taps[1] * pltpu.roll(here, depth - 1, 1)
                + taps[2] * pltpu.roll(here, 2, 1)
                + taps[3] * pltpu.roll(here, depth - 2, 1)
            )
            m = [med(k, med_at + i)[b : b + size, :] for k in range(3)]
            value = 2.0 * here - old(old_at + i)[b : b + size, :]
            value = value + m[across] * plane_sum + m[1 - across] * row_sum + m[2] * depth_sum
            if extra is not None:
                value = value + extra(i, b, size)
            new[i, new_pad + b : new_pad + b + size, :] = value

    each(count, rows, one)


def shoot(new, pad, first, count, plane, row, depth_at, amount):
    local = plane - first

    @pl.when((local >= 0) & (local < count))
    def _():
        lane = lax.broadcasted_iota(jnp.int32, (1, new.shape[2]), 1)
        spot = (pl.ds(local, 1), pl.ds(pad + row, 1), slice(None))
        new[spot] = new[spot] + jnp.where(lane == depth_at, -amount, 0.0)[None]


def surface_at(surf, first, step, steps):
    def extra(i, b, size):
        held = surf(first + i // SLAB)[b : b + size, :]
        depth = held.shape[1]
        lane = lax.broadcasted_iota(jnp.int32, (size, depth), 1)
        total = jnp.zeros_like(held)
        shift = (i % SLAB) * steps + step
        if isinstance(shift, int):
            return jnp.where(lane == 0, pltpu.roll(held, (depth - shift) % depth, 1), 0.0)
        for s in range(SLAB):
            moved = pltpu.roll(held, (depth - s * steps - step) % depth, 1)
            total = jnp.where((lane == 0) & (i % SLAB == s), moved, total)
        return total

    return extra


def clear(window, pad, rows):
    count, _, depth = window.shape
    zero = jnp.zeros((count, pad, depth), jnp.float32)
    window[:, 0:pad, :] = zero
    window[:, pad + rows :, :] = zero


def place(window, at, pad, value):
    window[at, pad : pad + value.shape[0], :] = value


def own_planes(refs, window, pad, base, at, core):
    for src, q in ((refs[0], core), (refs[1], 1 - core)):
        for p in range(SLAB):
            place(window, base + SLAB * q + p, pad, src[at + p])


def side_planes(refs, window, pad, base, ats, core):
    for src, side in ((refs[0], core), (refs[1], 1 - core)):
        for n, at in enumerate(ats):
            for p in range(SLAB):
                place(window, base * side + SLAB * n + p, pad, src[at + p])


def now_window(refs, window, kind, core):
    own_planes(refs[:2], window, EDGE, CHIP, SLAB * kind, core)
    side_planes(refs[2:], window, EDGE, 2 * CHIP, (SLAB * kind, SLAB * (2 + kind)), core)


def rim_window(refs, window, kind, core):
    own_planes(refs[:2], window, 0, SLAB, SLAB * (2 + kind), core)
    side_planes(refs[2:], window, 0, SLAB + CHIP, (SLAB * (4 + kind),), core)


def two_steps(now, old, med, new, edge, across, surface, shots):
    rows = edge.shape[1]
    count = old.shape[0]
    held = count // SLAB

    def medium(k, i):
        return med[k][i]

    extra = [None if surface is None else surface_at(lambda i: surface[i], n, n, STEPS) for n in range(2)]
    clear(now, EDGE, rows)
    clear(new, EDGE, rows)
    advance(now, SLAB, lambda i: old[i], 0, medium, 0, new, EDGE, count, EDGE, rows, across, extra[0])
    if shots:
        first, plane, row, deep, amounts = shots
        shoot(new, EDGE, first, count, plane, row, deep, amounts[0])
    advance(
        new, SLAB, lambda i: now[CHIP + i, EDGE : EDGE + rows, :], 0, medium, SLAB, edge, 0,
        CHIP, EDGE, rows, across, extra[1],
    )
    if shots:
        shoot(edge, 0, first + SLAB, CHIP, plane, row, deep, amounts[1])


def fetched(pair, window, pad, count, at, core):
    rows = window.shape[1] - 2 * pad
    for src, q in ((pair[0], core), (pair[1], 1 - core)):
        for p in range(count):
            place(window, count * q + p, pad, src[pl.ds(at + p, rows, stride=FETCH), :])


def first_y(
    where, shot, wavelet, loc, sib, near, near_sib, got, got_sib, edge, carry,
    now_r, now_s, old_r, old_s, med_0, med_1, med_2, surf, new_r, new_s,
):
    core, chip = where[0], where[1]
    refs = (loc, sib, near, near_sib)
    rows = loc.shape[1]
    med = (med_0, med_1, med_2)
    now_window(refs, now_r, RCV, core)
    rim_window(refs, old_r, RCV, core)
    for k in range(3):
        rim_window(refs, med[k], 2 + k, core)
    for n, ref in enumerate(refs):
        flip = core if n % 2 == 0 else 1 - core
        surf[1 + flip if n < 2 else 3 * flip] = ref[ref.shape[0] - 1]
    fetched((got, got_sib), now_s, EDGE, HALF_NOW, 0, core)
    fetched((got, got_sib), old_s, 0, HALF_OLD, HALF_NOW, core)
    two_steps(now_r, old_r, med, new_r, edge.at[0], 1, surf, None)
    shots = (CHIP * chip - SLAB, shot[1], shot[0], shot[2], (wavelet[0], wavelet[1]))
    two_steps(now_s, old_s, med, new_s, edge.at[1], 1, None, shots)
    for i in range(SPAN):
        at = SLAB * core + i
        carry[i] = new_r[at, EDGE : EDGE + rows, :]
        carry[SPAN + i] = new_s[at, EDGE : EDGE + rows, :]
        for k in range(3):
            carry[SPAN * (2 + k) + i] = med[k][at]
    for i in range(3):
        carry[SPAN * 5 + i] = surf[core + i]


def first_x(
    where, shot, wavelet, loc, sib, near, near_sib, got, got_sib, edge, carry,
    now, old, med_0, med_1, med_2, new,
):
    core, chip = where[0], where[1]
    refs = (loc, sib, near, near_sib)
    rows = loc.shape[1]
    med = (med_0, med_1, med_2)
    now_window(refs, now, SRC, core)
    rim_window(refs, old, SRC, core)
    for k in range(3):
        fetched((got, got_sib), med[k], 0, HALF_OLD, HALF_NOW + HALF_OLD * (k + 1), core)
    shots = (CHIP * chip - SLAB, shot[0], shot[1], shot[2], (wavelet[0], wavelet[1]))
    two_steps(now, old, med, new, edge.at[0], 0, None, shots)
    for i in range(SPAN):
        at = SLAB * core + i
        carry[i] = new[at, EDGE : EDGE + rows, :]
        for k in range(3):
            carry[SPAN * (1 + k) + i] = med[k][at]


def last_steps(where, edges, n, now, old, med, new, end, across, surface, shots):
    core = where[0]
    edge, near, near_sib = edges
    rows = edge.shape[2]
    pad = (now.shape[1] - rows) // 2
    for window in (now, new, end):
        clear(window, pad, rows)
    for p in range(CHIP):
        place(now, CHIP + p, pad, edge[n, p])
        for src, side in ((near, core), (near_sib, 1 - core)):
            plane = jnp.where(where[2 + side] == 1, src[n, p], 0.0)
            place(now, 2 * CHIP * side + p, pad, plane)
    extra = [None if surface is None else surface_at(surface, s, 2 + s, STEPS) for s in range(2)]
    advance(now, SLAB * core + SLAB, old, 0, med, 0, new, pad, SPAN, pad, rows, across, extra[0])
    if shots:
        first, plane, row, deep, amounts = shots
        shoot(new, pad, first, SPAN, plane, row, deep, amounts[0])

    def older(i):
        return now[CHIP + SLAB * core + i, pad : pad + rows, :]

    advance(new, SLAB, older, 0, med, SLAB, end, pad, SLAB, pad, rows, across, extra[1])
    if shots:
        shoot(end, pad, first + SLAB, SLAB, plane, row, deep, amounts[1])


def finish(end, new, following, prior, sems, at):
    rows = following.shape[1]
    inner = pl.ds((end.shape[1] - rows) // 2, rows)
    copies = [
        pltpu.make_async_copy(end.at[:, inner], following, sems.at[at]),
        pltpu.make_async_copy(new.at[pl.ds(SLAB, SLAB), inner], prior, sems.at[at + 1]),
    ]
    for copy in copies:
        copy.start()
    return copies


def second_half(
    where, shot, wavelet, lag_order, edge, near, near_sib, carry, edge_x, near_x, sib_x, carry_x,
    src_next, src_prior, rcv_next, rcv_prior, image,
    now_r, now_s, now_x, new_r, new_s, new_x, end_r, end_s, end_x, planes, slot_of, sems,
):
    rows, depth = carry.shape[1:]
    lags = lag_order.shape[0]
    half = (lags - 1) // 2
    pad = (now_r.shape[1] - rows) // 2
    core, chip = where[0], where[1]

    def note(k, _):
        slot_of[lag_order[k]] = k
        return 0

    lax.fori_loop(0, lags, note, 0)

    def med(k, i):
        return carry[SPAN * (2 + k) + i]

    edges = (edge, near, near_sib)
    last_steps(
        where, edges, 0, now_r, lambda i: carry[i], med, new_r, end_r, 1,
        lambda i: carry[SPAN * 5 + i], None,
    )
    copies = finish(end_r, new_r, rcv_next, rcv_prior, sems, lags)
    first = CHIP * chip + SLAB * core - SLAB
    last_steps(
        where, edges, 1, now_s, lambda i: carry[SPAN + i], med, new_s, end_s, 1, None,
        (first, shot[1], shot[0], shot[2], (wavelet[2], wavelet[3])),
    )
    last_steps(
        where, (edge_x, near_x, sib_x), 0, now_x, lambda i: carry_x[i],
        lambda k, i: carry_x[SPAN * (1 + k) + i], new_x, end_x, 0, None,
        (first, shot[0], shot[1], shot[2], (wavelet[2], wavelet[3])),
    )
    copies += finish(end_x, new_x, src_next, src_prior, sems, lags + 2)
    own = CHIP + SLAB * core
    for slot in range(lags):
        lag = slot - half
        for p in range(SLAB):
            for b in range(0, rows, 8):
                if b + 8 <= abs(lag) or b >= rows - abs(lag):
                    planes[slot, p, b : b + 8, :] = jnp.zeros((8, depth), jnp.float32)
                    continue
                back, ahead = pad + b - lag, pad + b + lag
                planes[slot, p, b : b + 8, :] = (
                    now_s[own + p, back : back + 8, :] * now_r[own + p, ahead : ahead + 8, :]
                    + end_s[p, back : back + 8, :] * end_r[p, ahead : ahead + 8, :]
                )
        copies.append(
            pltpu.make_async_copy(planes.at[slot], image.at[slot_of[slot]], sems.at[slot])
        )
        copies[-1].start()
    for copy in copies:
        copy.wait()


def on_device(src_now, src_old, rcv_now, rcv_old, medium, wavelet, shot, traces, rec_x, lag_order):
    devices = lax.axis_size("wide")
    chips = devices // 2
    slab, rows, depth = src_now.shape
    assert slab == SLAB and rcv_now.shape == (SLAB, depth, rows) and wavelet.shape[0] == STEPS
    assert rows % 8 == 0 and rows == SLAB * devices
    lags = lag_order.shape[0]
    half = (lags - 1) // 2
    device = lax.axis_index("wide")
    chip, core = device // 2, device % 2
    last = chips - 1
    turning = chip == jnp.where(core == 0, last, 0)
    where = jnp.stack([core, chip, chip > 0, chip < last]).astype(jnp.int32)
    swap = [(i, i ^ 1) for i in range(devices)]
    order = [*range(0, devices, 2), *range(devices - 1, 0, -2)]
    ring = list(zip(order, order[1:] + order[:1]))

    def turned(x):
        return jnp.swapaxes(x, -1, -2)

    rcv_now, rcv_old, medium, traces = map(turned, (rcv_now, rcv_old, medium, traces))
    wide, loc = call(
        gather,
        (src_now, src_old, rcv_now, rcv_old, medium, traces, rec_x),
        [(5 * SLAB, rows + 2 * EDGE, depth), (7 * SLAB + 1, rows, depth)],
        [traces.shape],
        0,
        [pltpu.VMEM(rec_x.shape, jnp.int32), pltpu.SemaphoreType.DMA((14,))],
        far_in=True,
    )
    (send,) = call(pack, (wide,), [(devices, SLAB * FETCH, depth)], [], 0)
    got = lax.all_to_all(send, "wide", 0, 0, tiled=True).reshape(-1, depth)
    sib = lax.ppermute(loc, "wide", swap)
    low, high = jnp.where(core == 0, loc, sib), jnp.where(core == 0, sib, loc)
    rim = jnp.where(core == 0, high[2 * SLAB :], low[2 * SLAB :])
    ours = jnp.concatenate([low[: 2 * SLAB], high[: 2 * SLAB], rim])
    near = lax.ppermute(jnp.where(turning, 0.0, ours), "wide", ring)
    near_sib = lax.ppermute(near, "wide", swap)
    got_sib = lax.ppermute(got, "wide", swap)

    window, narrow = 3 * CHIP, 2 * CHIP
    padded, plain = (window, rows + 2 * EDGE, depth), (narrow, rows, depth)
    edge_y, carry_y = call(
        first_y,
        (where, shot, wavelet, loc, sib, near, near_sib, got, got_sib),
        [(2, CHIP, rows, depth), (SPAN * 5 + 3, rows, depth)],
        [padded] * 2 + [plain] * 5 + [(4, rows, depth)] + [(narrow, *padded[1:])] * 2,
        3,
    )
    mid_y = lax.ppermute(edge_y, "wide", ring)
    mid_y_sib = lax.ppermute(mid_y, "wide", swap)
    edge_x, carry_x = call(
        first_x,
        (where, shot, wavelet, loc, sib, near, near_sib, got, got_sib),
        [(1, CHIP, rows, depth), (SPAN * 4, rows, depth)],
        [padded] + [plain] * 4 + [(narrow, *padded[1:])],
        3,
    )
    mid_x = lax.ppermute(edge_x, "wide", ring)
    mid_x_sib = lax.ppermute(mid_x, "wide", swap)

    field = (SLAB, rows, depth)
    pad = -(-max(half, 2) // 8) * 8
    padded = (rows + 2 * pad, depth)
    src_next, src_prior, rcv_next, rcv_prior, image = call(
        second_half,
        (where, shot, wavelet, lag_order, edge_y, mid_y, mid_y_sib, carry_y)
        + (edge_x, mid_x, mid_x_sib, carry_x),
        [field] * 4 + [(lags, *field)],
        [(window, *padded)] * 3 + [(SPAN, *padded)] * 3 + [(SLAB, *padded)] * 3 + [(lags, *field)],
        4,
        [pltpu.SMEM((lags,), jnp.int32), pltpu.SemaphoreType.DMA((lags + 4,))],
        far_out=range(5),
    )
    return src_next, src_prior, turned(rcv_next), turned(rcv_prior), turned(image)


def solution(mesh):
    return jax.shard_map(
        on_device,
        mesh=mesh,
        in_specs=(
            P("wide", "shots", None),
            P("wide", "shots", None),
            P("wide", "shots", None),
            P("wide", "shots", None),
            P(None, "wide", None, None),
            P(),
            P("shots"),
            P("wide", "shots", None),
            P("wide", "shots"),
            P(),
        ),
        out_specs=(
            P("wide", "shots", None),
            P("wide", "shots", None),
            P("wide", "shots", None),
            P("wide", "shots", None),
            P("shots", "wide", None, None),
        ),
        check_vma=False,
    )
```

```python
import functools

import jax
import jax.numpy as jnp
from jax import lax
from jax.experimental import pallas as pl
from jax.experimental.pallas import tpu as pltpu
from jax.sharding import PartitionSpec as P

SLAB, CHIP, STEPS, EDGE = 2, 4, 4, 8
NEAR, FAR = 4.0 / 3.0, -1.0 / 12.0
RCV, SRC = 0, 1
SPAN = 3 * SLAB
HALF_NOW = (CHIP + 2 * CHIP) // 2
HALF_OLD = (CHIP + CHIP) // 2
FETCH = 24

VMEM = pl.BlockSpec(memory_space=pltpu.VMEM)
HBM = pl.BlockSpec(memory_space=pltpu.HBM)


def call(kernel, operands, outs, scratch, held=(), far=0, far_out=()):
    size = sum(4 * o.size for o in operands)
    size += sum(4 * functools.reduce(lambda a, b: a * b, s) for s in (*outs, *scratch))
    distant = [pltpu.with_memory_space_constraint(o, pltpu.HBM) for o in operands[:far]]
    return pl.pallas_call(
        kernel,
        out_shape=[jax.ShapeDtypeStruct(s, jnp.float32) for s in outs],
        in_specs=[HBM] * far + [VMEM] * (len(operands) - far),
        out_specs=[HBM if n in far_out else VMEM for n in range(len(outs))],
        scratch_shapes=[pltpu.VMEM(s, jnp.float32) for s in scratch] + list(held),
        compiler_params=pltpu.CompilerParams(vmem_limit_bytes=size + size // 4 + (8 << 20)),
    )(*distant, *operands[far:])


def position():
    device = lax.axis_index("wide")
    return lax.rem(device, 2), lax.div(device, 2)


def each(count, rows, body):
    if rows <= 32:
        for i in range(count):
            body(i)
    else:
        lax.fori_loop(0, count, lambda i, _: (body(i), 0)[1], 0)


def blocks(rows):
    size = min(rows, 32)
    return [(b, size) for b in range(0, rows, size)]


def gather(
    src_now, src_old, rcv_now, rcv_old, med, traces, rec_x, shot, wavelet,
    wide, loc, amount, spot, traces_in, rec_in, shot_in, wavelet_in, sems,
):
    rows, depth = src_now.shape[1:]
    steps, cells = traces.shape[1], loc.shape[1]
    inner = pl.ds(EDGE, rows)
    pairs = [(traces, traces_in), (rec_x, rec_in), (shot, shot_in), (wavelet, wavelet_in)]
    for n, own in enumerate((rcv_now, src_now, rcv_old, src_old)):
        pairs.append((own, loc.at[pl.ds(n * SLAB, SLAB)]))
    pairs += [(med.at[k], loc.at[pl.ds((4 + k) * SLAB, SLAB)]) for k in range(3)]
    for n, own in enumerate((src_now, src_old, med.at[0], med.at[1], med.at[2])):
        pairs.append((own, wide.at[pl.ds(n * SLAB, SLAB), inner]))
    copies = [pltpu.make_async_copy(a, b, sems.at[n]) for n, (a, b) in enumerate(pairs)]
    for copy in copies:
        copy.start()
    clear(wide, EDGE, rows)
    for copy in copies[:2]:
        copy.wait()
    lane = lax.broadcasted_iota(jnp.int32, (cells, depth), 1)
    place = lax.broadcasted_iota(jnp.int32, (cells, rec_x.shape[1]), 0)
    surface = jnp.zeros((cells, depth), jnp.float32)
    for h in range(SLAB):
        hit = rec_in[h : h + 1, :] == place
        for s in range(steps):
            column = jnp.sum(jnp.where(hit, traces_in[h, s : s + 1, :], 0.0), axis=1, keepdims=True)
            surface = jnp.where(lane == steps * h + s, column, surface)
    loc[7 * SLAB] = surface
    for copy in copies[2:4]:
        copy.wait()
    core, chip = position()
    own = CHIP * chip + SLAB * core
    first = (CHIP * chip - SLAB, CHIP * chip, own - SLAB, own)
    plane = lax.broadcasted_iota(jnp.int32, amount.shape[2:], 0)
    row = lax.broadcasted_iota(jnp.int32, (cells, depth), 0)
    for chain, (at_plane, at_row) in enumerate(((1, 0), (0, 1))):
        here = (row == shot_in[at_row]) & (lane == shot_in[2])
        spot[chain] = jnp.where(here, 1.0, 0.0)
        for step in range(steps):
            hit = plane == shot_in[at_plane] - first[step]
            amount[chain, step] = jnp.where(hit, -wavelet_in[step], 0.0)
    for copy in copies[4:]:
        copy.wait()


def pack(wide, send):
    for j in range(send.shape[0]):
        chip, core = divmod(j, 2)
        now_at = EDGE + CHIP * chip - CHIP + HALF_NOW * core
        old_at = EDGE + CHIP * chip - SLAB + HALF_OLD * core
        for h in range(SLAB):
            at = FETCH * h
            send[j, at : at + HALF_NOW, :] = wide[h, now_at : now_at + HALF_NOW, :]
            for k in range(4):
                at = FETCH * h + HALF_NOW + HALF_OLD * k
                plane = SLAB * (k + 1) + h
                send[j, at : at + HALF_OLD, :] = wide[plane, old_at : old_at + HALF_OLD, :]


def advance(now, now_at, old, old_at, med, med_at, new, new_pad, count, pad, rows, across, extra):
    depth = now.shape[2]
    lane = lax.broadcasted_iota(jnp.int32, (8, depth), 1)
    weight = [
        jnp.where(lane >= 1, NEAR, 0.0),
        jnp.where(lane < depth - 1, NEAR, 0.0),
        jnp.where(lane >= 2, FAR, 0.0),
        jnp.where(lane < depth - 2, FAR, 0.0),
    ]

    def one(i):
        w = now_at + i
        for b, size in blocks(rows):
            taps = [jnp.concatenate([t] * (size // 8), axis=0) for t in weight]

            def at(plane, shift):
                return now[plane, pad + b + shift : pad + b + shift + size, :]

            here = at(w, 0)
            centre = -2.5 * here
            plane_sum = (
                centre
                + NEAR * (at(w - 1, 0) + at(w + 1, 0))
                + FAR * (at(w - 2, 0) + at(w + 2, 0))
            )
            row_sum = (
                centre
                + NEAR * (at(w, -1) + at(w, 1))
                + FAR * (at(w, -2) + at(w, 2))
            )
            depth_sum = (
                centre
                + taps[0] * pltpu.roll(here, 1, 1)
                + taps[1] * pltpu.roll(here, depth - 1, 1)
                + taps[2] * pltpu.roll(here, 2, 1)
                + taps[3] * pltpu.roll(here, depth - 2, 1)
            )
            m = [med(k, med_at + i)[b : b + size, :] for k in range(3)]
            value = 2.0 * here - old(old_at + i)[b : b + size, :]
            value = value + m[across] * plane_sum + m[1 - across] * row_sum + m[2] * depth_sum
            if extra is not None:
                value = value + extra(i, b, size)
            new[i, new_pad + b : new_pad + b + size, :] = value

    each(count, rows, one)


def shot_at(amount, spot, chain, step):
    def extra(i, b, size):
        return amount[chain, step, pl.ds(i, 1), :] * spot[chain, b : b + size, :]

    return extra


def surface_at(surf, first, step, steps):
    def extra(i, b, size):
        held = surf(first + i // SLAB)[b : b + size, :]
        depth = held.shape[1]
        lane = lax.broadcasted_iota(jnp.int32, (size, depth), 1)
        total = jnp.zeros_like(held)
        shift = (i % SLAB) * steps + step
        if isinstance(shift, int):
            return jnp.where(lane == 0, pltpu.roll(held, (depth - shift) % depth, 1), 0.0)
        for s in range(SLAB):
            moved = pltpu.roll(held, (depth - s * steps - step) % depth, 1)
            total = jnp.where((lane == 0) & (i % SLAB == s), moved, total)
        return total

    return extra


def clear(window, pad, rows):
    count, _, depth = window.shape
    zero = jnp.zeros((count, pad, depth), jnp.float32)
    window[:, 0:pad, :] = zero
    window[:, pad + rows :, :] = zero


def place(window, at, pad, value):
    window[at, pad : pad + value.shape[0], :] = value


def own_planes(refs, window, pad, base, at, core):
    for src, q in ((refs[0], core), (refs[1], 1 - core)):
        for p in range(SLAB):
            place(window, base + SLAB * q + p, pad, src[at + p])


def side_planes(refs, window, pad, base, ats, core):
    for src, side in ((refs[0], core), (refs[1], 1 - core)):
        for n, at in enumerate(ats):
            for p in range(SLAB):
                place(window, base * side + SLAB * n + p, pad, src[at + p])


def now_window(refs, window, kind, core):
    own_planes(refs[:2], window, EDGE, CHIP, SLAB * kind, core)
    side_planes(refs[2:], window, EDGE, 2 * CHIP, (SLAB * kind, SLAB * (2 + kind)), core)


def rim_window(refs, window, kind, core):
    own_planes(refs[:2], window, 0, SLAB, SLAB * (2 + kind), core)
    side_planes(refs[2:], window, 0, SLAB + CHIP, (SLAB * (4 + kind),), core)


def two_steps(now, old, med, new, edge, across, extras):
    rows = edge.shape[1]
    count = old.shape[0]

    def medium(k, i):
        return med[k][i]

    clear(now, EDGE, rows)
    clear(new, EDGE, rows)
    advance(now, SLAB, lambda i: old[i], 0, medium, 0, new, EDGE, count, EDGE, rows, across, extras[0])
    advance(
        new, SLAB, lambda i: now[CHIP + i, EDGE : EDGE + rows, :], 0, medium, SLAB, edge, 0,
        CHIP, EDGE, rows, across, extras[1],
    )


def fetched(pair, window, pad, count, at, core):
    rows = window.shape[1] - 2 * pad
    for src, q in ((pair[0], core), (pair[1], 1 - core)):
        for p in range(count):
            place(window, count * q + p, pad, src[pl.ds(at + p, rows, stride=FETCH), :])


def first_y(
    amount, spot, loc, sib, near, near_sib, got, got_sib, edge, carry,
    now_r, now_s, old_r, old_s, med_0, med_1, med_2, surf, new_r, new_s,
):
    core, _ = position()
    refs = (loc, sib, near, near_sib)
    rows = loc.shape[1]
    med = (med_0, med_1, med_2)
    now_window(refs, now_r, RCV, core)
    rim_window(refs, old_r, RCV, core)
    for k in range(3):
        rim_window(refs, med[k], 2 + k, core)
    for n, ref in enumerate(refs):
        flip = core if n % 2 == 0 else 1 - core
        surf[1 + flip if n < 2 else 3 * flip] = ref[ref.shape[0] - 1]
    fetched((got, got_sib), now_s, EDGE, HALF_NOW, 0, core)
    fetched((got, got_sib), old_s, 0, HALF_OLD, HALF_NOW, core)
    receivers = [surface_at(lambda i: surf[i], n, n, STEPS) for n in range(2)]
    two_steps(now_r, old_r, med, new_r, edge.at[0], 1, receivers)
    shots = [shot_at(amount, spot, 0, n) for n in range(2)]
    two_steps(now_s, old_s, med, new_s, edge.at[1], 1, shots)
    for i in range(SPAN):
        at = SLAB * core + i
        carry[i] = new_r[at, EDGE : EDGE + rows, :]
        carry[SPAN + i] = new_s[at, EDGE : EDGE + rows, :]
        for k in range(3):
            carry[SPAN * (2 + k) + i] = med[k][at]
    for i in range(3):
        carry[SPAN * 5 + i] = surf[core + i]


def first_x(
    amount, spot, loc, sib, near, near_sib, got, got_sib, edge, carry,
    now, old, med_0, med_1, med_2, new,
):
    core, _ = position()
    refs = (loc, sib, near, near_sib)
    rows = loc.shape[1]
    med = (med_0, med_1, med_2)
    now_window(refs, now, SRC, core)
    rim_window(refs, old, SRC, core)
    for k in range(3):
        fetched((got, got_sib), med[k], 0, HALF_OLD, HALF_NOW + HALF_OLD * (k + 1), core)
    two_steps(now, old, med, new, edge.at[0], 0, [shot_at(amount, spot, 1, n) for n in range(2)])
    for i in range(SPAN):
        at = SLAB * core + i
        carry[i] = new[at, EDGE : EDGE + rows, :]
        for k in range(3):
            carry[SPAN * (1 + k) + i] = med[k][at]


def last_steps(last, edges, n, now, old, med, new, end, across, extras):
    core, chip = position()
    edge, near, near_sib = edges
    rows = edge.shape[2]
    pad = (now.shape[1] - rows) // 2
    for window in (now, new, end):
        clear(window, pad, rows)
    for p in range(CHIP):
        place(now, CHIP + p, pad, edge[n, p])
        for src, side in ((near, core), (near_sib, 1 - core)):
            beyond = chip + 2 * side - 1
            plane = jnp.where((beyond >= 0) & (beyond <= last), src[n, p], 0.0)
            place(now, 2 * CHIP * side + p, pad, plane)
    advance(now, SLAB * core + SLAB, old, 0, med, 0, new, pad, SPAN, pad, rows, across, extras[0])

    def older(i):
        return now[CHIP + SLAB * core + i, pad : pad + rows, :]

    advance(new, SLAB, older, 0, med, SLAB, end, pad, SLAB, pad, rows, across, extras[1])


def finish(end, new, following, prior, sems, at):
    rows = following.shape[1]
    inner = pl.ds((end.shape[1] - rows) // 2, rows)
    copies = [
        pltpu.make_async_copy(end.at[:, inner], following, sems.at[at]),
        pltpu.make_async_copy(new.at[pl.ds(SLAB, SLAB), inner], prior, sems.at[at + 1]),
    ]
    for copy in copies:
        copy.start()
    return copies


def second_half(
    last, lag_order, amount, spot, edge, near, near_sib, carry, edge_x, near_x, sib_x, carry_x,
    src_next, src_prior, rcv_next, rcv_prior, image,
    now_r, now_s, now_x, new_r, new_s, new_x, end_r, end_s, end_x, planes, order, slot_of, sems,
):
    rows, depth = carry.shape[1:]
    lags = lag_order.shape[0]
    half = (lags - 1) // 2
    pad = (now_r.shape[1] - rows) // 2
    core, _ = position()
    lags_in = pltpu.make_async_copy(lag_order, order, sems.at[lags + 4])
    lags_in.start()

    def med(k, i):
        return carry[SPAN * (2 + k) + i]

    edges = (edge, near, near_sib)
    receivers = [surface_at(lambda i: carry[SPAN * 5 + i], n, 2 + n, STEPS) for n in range(2)]
    last_steps(last, edges, 0, now_r, lambda i: carry[i], med, new_r, end_r, 1, receivers)
    copies = finish(end_r, new_r, rcv_next, rcv_prior, sems, lags)
    shots = [shot_at(amount, spot, 0, 2 + n) for n in range(2)]
    last_steps(last, edges, 1, now_s, lambda i: carry[SPAN + i], med, new_s, end_s, 1, shots)
    shots = [shot_at(amount, spot, 1, 2 + n) for n in range(2)]
    last_steps(
        last, (edge_x, near_x, sib_x), 0, now_x, lambda i: carry_x[i],
        lambda k, i: carry_x[SPAN * (1 + k) + i], new_x, end_x, 0, shots,
    )
    copies += finish(end_x, new_x, src_next, src_prior, sems, lags + 2)
    lags_in.wait()
    for k in range(lags):
        slot_of[order[k]] = k
    own = CHIP + SLAB * core
    for slot in range(lags):
        lag = slot - half
        for p in range(SLAB):
            for b in range(0, rows, 8):
                if b + 8 <= abs(lag) or b >= rows - abs(lag):
                    planes[slot, p, b : b + 8, :] = jnp.zeros((8, depth), jnp.float32)
                    continue
                back, ahead = pad + b - lag, pad + b + lag
                planes[slot, p, b : b + 8, :] = (
                    now_s[own + p, back : back + 8, :] * now_r[own + p, ahead : ahead + 8, :]
                    + end_s[p, back : back + 8, :] * end_r[p, ahead : ahead + 8, :]
                )
        copies.append(
            pltpu.make_async_copy(planes.at[slot], image.at[slot_of[slot]], sems.at[slot])
        )
        copies[-1].start()
    for copy in copies:
        copy.wait()


def on_device(src_now, src_old, rcv_now, rcv_old, medium, wavelet, shot, traces, rec_x, lag_order):
    devices = lax.axis_size("wide")
    chips = devices // 2
    slab, rows, depth = src_now.shape
    assert slab == SLAB and rcv_now.shape == (SLAB, depth, rows) and wavelet.shape[0] == STEPS
    assert rows % 8 == 0 and rows == SLAB * devices
    lags = lag_order.shape[0]
    half = (lags - 1) // 2
    device = lax.axis_index("wide")
    chip, core = device // 2, device % 2
    last = chips - 1
    turning = chip == jnp.where(core == 0, last, 0)
    swap = [(i, i ^ 1) for i in range(devices)]
    order = [*range(0, devices, 2), *range(devices - 1, 0, -2)]
    ring = list(zip(order, order[1:] + order[:1]))

    def turned(x):
        return jnp.swapaxes(x, -1, -2)

    rcv_now, rcv_old, medium, traces = map(turned, (rcv_now, rcv_old, medium, traces))
    scalars = [pltpu.SMEM(shot.shape, jnp.int32), pltpu.SMEM(wavelet.shape, jnp.float32)]
    wide, loc, amount, spot = call(
        gather,
        (src_now, src_old, rcv_now, rcv_old, medium, traces, rec_x, shot, wavelet),
        [(5 * SLAB, rows + 2 * EDGE, depth), (7 * SLAB + 1, rows, depth)]
        + [(2, STEPS, 2 * CHIP, depth), (2, rows, depth)],
        [traces.shape],
        [pltpu.VMEM(rec_x.shape, jnp.int32), *scalars, pltpu.SemaphoreType.DMA((16,))],
        far=9,
    )
    (send,) = call(pack, (wide,), [(devices, SLAB * FETCH, depth)], [])
    got = lax.all_to_all(send, "wide", 0, 0, tiled=True).reshape(-1, depth)
    sib = lax.ppermute(loc, "wide", swap)
    low, high = jnp.where(core == 0, loc, sib), jnp.where(core == 0, sib, loc)
    rim = jnp.where(core == 0, high[2 * SLAB :], low[2 * SLAB :])
    ours = jnp.concatenate([low[: 2 * SLAB], high[: 2 * SLAB], rim])
    near = lax.ppermute(jnp.where(turning, 0.0, ours), "wide", ring)
    near_sib = lax.ppermute(near, "wide", swap)
    got_sib = lax.ppermute(got, "wide", swap)

    window, narrow = 3 * CHIP, 2 * CHIP
    padded, plain = (window, rows + 2 * EDGE, depth), (narrow, rows, depth)
    edge_y, carry_y = call(
        first_y,
        (amount, spot, loc, sib, near, near_sib, got, got_sib),
        [(2, CHIP, rows, depth), (SPAN * 5 + 3, rows, depth)],
        [padded] * 2 + [plain] * 5 + [(4, rows, depth)] + [(narrow, *padded[1:])] * 2,
    )
    mid_y = lax.ppermute(edge_y, "wide", ring)
    mid_y_sib = lax.ppermute(mid_y, "wide", swap)
    edge_x, carry_x = call(
        first_x,
        (amount, spot, loc, sib, near, near_sib, got, got_sib),
        [(1, CHIP, rows, depth), (SPAN * 4, rows, depth)],
        [padded] + [plain] * 4 + [(narrow, *padded[1:])],
    )
    mid_x = lax.ppermute(edge_x, "wide", ring)
    mid_x_sib = lax.ppermute(mid_x, "wide", swap)

    field = (SLAB, rows, depth)
    pad = -(-max(half, 2) // 8) * 8
    padded = (rows + 2 * pad, depth)
    src_next, src_prior, rcv_next, rcv_prior, image = call(
        functools.partial(second_half, last),
        (lag_order, amount, spot, edge_y, mid_y, mid_y_sib, carry_y)
        + (edge_x, mid_x, mid_x_sib, carry_x),
        [field] * 4 + [(lags, *field)],
        [(window, *padded)] * 3 + [(SPAN, *padded)] * 3 + [(SLAB, *padded)] * 3 + [(lags, *field)],
        [pltpu.SMEM((lags,), jnp.int32)] * 2 + [pltpu.SemaphoreType.DMA((lags + 5,))],
        far=1,
        far_out=range(5),
    )
    return src_next, src_prior, turned(rcv_next), turned(rcv_prior), turned(image)


def solution(mesh):
    return jax.shard_map(
        on_device,
        mesh=mesh,
        in_specs=(
            P("wide", "shots", None),
            P("wide", "shots", None),
            P("wide", "shots", None),
            P("wide", "shots", None),
            P(None, "wide", None, None),
            P(),
            P("shots"),
            P("wide", "shots", None),
            P("wide", "shots"),
            P(),
        ),
        out_specs=(
            P("wide", "shots", None),
            P("wide", "shots", None),
            P("wide", "shots", None),
            P("wide", "shots", None),
            P("shots", "wide", None, None),
        ),
        check_vma=False,
    )
```

```python
import functools

import jax
import jax.numpy as jnp
from jax import lax
from jax.experimental import pallas as pl
from jax.experimental.pallas import tpu as pltpu
from jax.sharding import PartitionSpec as P

SLAB, CHIP, STEPS, EDGE = 2, 4, 4, 8
NEAR, FAR = 4.0 / 3.0, -1.0 / 12.0
RCV, SRC = 0, 1
SPAN = 3 * SLAB
HALF_NOW = (CHIP + 2 * CHIP) // 2
HALF_OLD = (CHIP + CHIP) // 2
FETCH = 24
REST = 8

VMEM = pl.BlockSpec(memory_space=pltpu.VMEM)
HBM = pl.BlockSpec(memory_space=pltpu.HBM)


def call(kernel, operands, outs, scratch, held=(), far=0, far_out=()):
    size = sum(4 * o.size for o in operands)
    size += sum(4 * functools.reduce(lambda a, b: a * b, s) for s in (*outs, *scratch))
    distant = [pltpu.with_memory_space_constraint(o, pltpu.HBM) for o in operands[:far]]
    return pl.pallas_call(
        kernel,
        out_shape=[jax.ShapeDtypeStruct(s, jnp.float32) for s in outs],
        in_specs=[HBM] * far + [VMEM] * (len(operands) - far),
        out_specs=[HBM if n in far_out else VMEM for n in range(len(outs))],
        scratch_shapes=[pltpu.VMEM(s, jnp.float32) for s in scratch] + list(held),
        compiler_params=pltpu.CompilerParams(vmem_limit_bytes=size + size // 4 + (8 << 20)),
    )(*distant, *operands[far:])


def position():
    device = lax.axis_index("wide")
    return lax.rem(device, 2), lax.div(device, 2)


def each(count, rows, body):
    if rows <= 32:
        for i in range(count):
            body(i)
    else:
        lax.fori_loop(0, count, lambda i, _: (body(i), 0)[1], 0)


def blocks(rows):
    size = min(rows, 32)
    return [(b, size) for b in range(0, rows, size)]


def gather(
    src_now, src_old, rcv_now, rcv_old, med, traces, rec_x, shot, wavelet,
    wide, loc, amount, spot, traces_in, rec_in, shot_in, wavelet_in, sems,
):
    rows, depth = src_now.shape[1:]
    steps, cells = traces.shape[1], loc.shape[1]
    inner = pl.ds(EDGE, rows)
    pairs = [(traces, traces_in), (rec_x, rec_in), (shot, shot_in), (wavelet, wavelet_in)]
    for n, own in enumerate((rcv_now, src_now, rcv_old, src_old)):
        pairs.append((own, loc.at[pl.ds(n * SLAB, SLAB)]))
    pairs += [(med.at[k], loc.at[pl.ds((4 + k) * SLAB, SLAB)]) for k in range(3)]
    for n, own in enumerate((src_now, src_old, med.at[0], med.at[1], med.at[2])):
        pairs.append((own, wide.at[pl.ds(n * SLAB, SLAB), inner]))
    copies = [pltpu.make_async_copy(a, b, sems.at[n]) for n, (a, b) in enumerate(pairs)]
    for copy in copies:
        copy.start()
    clear(wide, EDGE, rows)
    for copy in copies[:2]:
        copy.wait()
    lane = lax.broadcasted_iota(jnp.int32, (cells, depth), 1)
    place = lax.broadcasted_iota(jnp.int32, (cells, rec_x.shape[1]), 0)
    surface = jnp.zeros((cells, depth), jnp.float32)
    for h in range(SLAB):
        hit = rec_in[h : h + 1, :] == place
        for s in range(steps):
            column = jnp.sum(jnp.where(hit, traces_in[h, s : s + 1, :], 0.0), axis=1, keepdims=True)
            surface = jnp.where(lane == steps * h + s, column, surface)
    loc[7 * SLAB] = surface
    for copy in copies[2:4]:
        copy.wait()
    core, chip = position()
    own = CHIP * chip + SLAB * core
    first = (CHIP * chip - SLAB, CHIP * chip, own - SLAB, own)
    plane = lax.broadcasted_iota(jnp.int32, amount.shape[2:], 0)
    row = lax.broadcasted_iota(jnp.int32, (cells, depth), 0)
    for chain, (at_plane, at_row) in enumerate(((1, 0), (0, 1))):
        here = (row == shot_in[at_row]) & (lane == shot_in[2])
        spot[chain] = jnp.where(here, 1.0, 0.0)
        for step in range(steps):
            hit = plane == shot_in[at_plane] - first[step]
            amount[chain, step] = jnp.where(hit, -wavelet_in[step], 0.0)
    for copy in copies[4:]:
        copy.wait()


def pack(wide, send):
    for j in range(send.shape[0]):
        chip, core = divmod(j, 2)
        now_at = EDGE + CHIP * chip - CHIP + HALF_NOW * core
        old_at = EDGE + CHIP * chip - SLAB + HALF_OLD * core
        for h in range(SLAB):
            at = FETCH * h
            send[j, at : at + HALF_NOW, :] = wide[h, now_at : now_at + HALF_NOW, :]
            for k in range(4):
                at = FETCH * h + REST + HALF_OLD * k
                plane = SLAB * (k + 1) + h
                send[j, at : at + HALF_OLD, :] = wide[plane, old_at : old_at + HALF_OLD, :]


def advance(now, now_at, old, old_at, med, med_at, new, new_pad, count, pad, rows, across, extra):
    depth = now.shape[2]
    lane = lax.broadcasted_iota(jnp.int32, (8, depth), 1)
    weight = [
        jnp.where(lane >= 1, NEAR, 0.0),
        jnp.where(lane < depth - 1, NEAR, 0.0),
        jnp.where(lane >= 2, FAR, 0.0),
        jnp.where(lane < depth - 2, FAR, 0.0),
    ]

    def one(i):
        w = now_at + i
        for b, size in blocks(rows):
            taps = [jnp.concatenate([t] * (size // 8), axis=0) for t in weight]

            def at(plane, shift):
                return now[plane, pad + b + shift : pad + b + shift + size, :]

            here = at(w, 0)
            centre = -2.5 * here
            plane_sum = (
                centre
                + NEAR * (at(w - 1, 0) + at(w + 1, 0))
                + FAR * (at(w - 2, 0) + at(w + 2, 0))
            )
            row_sum = (
                centre
                + NEAR * (at(w, -1) + at(w, 1))
                + FAR * (at(w, -2) + at(w, 2))
            )
            depth_sum = (
                centre
                + taps[0] * pltpu.roll(here, 1, 1)
                + taps[1] * pltpu.roll(here, depth - 1, 1)
                + taps[2] * pltpu.roll(here, 2, 1)
                + taps[3] * pltpu.roll(here, depth - 2, 1)
            )
            m = [med(k, med_at + i)[b : b + size, :] for k in range(3)]
            value = 2.0 * here - old(old_at + i)[b : b + size, :]
            value = value + m[across] * plane_sum + m[1 - across] * row_sum + m[2] * depth_sum
            if extra is not None:
                value = value + extra(i, b, size)
            new[i, new_pad + b : new_pad + b + size, :] = value

    each(count, rows, one)


def shot_at(amount, spot, chain, step):
    def extra(i, b, size, at=0):
        return amount[chain, step, pl.ds(at + i, 1), :] * spot[chain, b : b + size, :]

    return extra


def surface_at(surf, first, step, steps):
    def extra(i, b, size, at=0):
        held = surf(first + lax.div(at, SLAB) + i // SLAB)[b : b + size, :]
        depth = held.shape[1]
        lane = lax.broadcasted_iota(jnp.int32, (size, depth), 1)
        if isinstance(i, int):
            shift = (i % SLAB) * steps + step
            return jnp.where(lane == 0, pltpu.roll(held, (depth - shift) % depth, 1), 0.0)
        total = jnp.zeros_like(held)
        for s in range(SLAB):
            moved = pltpu.roll(held, (depth - s * steps - step) % depth, 1)
            total = jnp.where((lane == 0) & (i % SLAB == s), moved, total)
        return total

    return extra


def clear(window, pad, rows):
    count, _, depth = window.shape
    zero = jnp.zeros((count, pad, depth), jnp.float32)
    window[:, 0:pad, :] = zero
    window[:, pad + rows :, :] = zero


def place(window, at, pad, value):
    window[at, pad : pad + value.shape[0], :] = value


def own_planes(refs, window, pad, base, at, core):
    for src, q in ((refs[0], core), (refs[1], 1 - core)):
        for p in range(SLAB):
            place(window, base + SLAB * q + p, pad, src[at + p])


def side_planes(refs, window, pad, base, ats, core):
    for src, side in ((refs[0], core), (refs[1], 1 - core)):
        for n, at in enumerate(ats):
            for p in range(SLAB):
                place(window, base * side + SLAB * n + p, pad, src[at + p])


def now_window(refs, window, kind, core):
    own_planes(refs[:2], window, EDGE, CHIP, SLAB * kind, core)
    side_planes(refs[2:], window, EDGE, 2 * CHIP, (SLAB * kind, SLAB * (2 + kind)), core)


def rim_window(refs, window, kind, core):
    own_planes(refs[:2], window, 0, SLAB, SLAB * (2 + kind), core)
    side_planes(refs[2:], window, 0, SLAB + CHIP, (SLAB * (4 + kind),), core)


def two_steps(now, old, med, new, edge, across, extras):
    rows = edge.shape[1]
    count = old.shape[0]

    def medium(k, i):
        return med[k][i]

    clear(now, EDGE, rows)
    clear(new, EDGE, rows)
    advance(now, SLAB, lambda i: old[i], 0, medium, 0, new, EDGE, count, EDGE, rows, across, extras[0])
    advance(
        new, SLAB, lambda i: now[CHIP + i, EDGE : EDGE + rows, :], 0, medium, SLAB, edge, 0,
        CHIP, EDGE, rows, across, extras[1],
    )


def fetched(pair, window, pad, count, at, core):
    rows = window.shape[1] - 2 * pad
    for src, q in ((pair[0], core), (pair[1], 1 - core)):
        for p in range(count):
            place(window, count * q + p, pad, src[pl.ds(at + p, rows, stride=FETCH), :])


def first_y(
    amount, spot, loc, sib, near, near_sib, got, got_sib, edge, carry,
    now_r, now_s, old_r, old_s, med_0, med_1, med_2, surf, new_r, new_s,
):
    core, _ = position()
    refs = (loc, sib, near, near_sib)
    rows = loc.shape[1]
    med = (med_0, med_1, med_2)
    now_window(refs, now_r, RCV, core)
    rim_window(refs, old_r, RCV, core)
    for k in range(3):
        rim_window(refs, med[k], 2 + k, core)
    for n, ref in enumerate(refs):
        flip = core if n % 2 == 0 else 1 - core
        surf[1 + flip if n < 2 else 3 * flip] = ref[ref.shape[0] - 1]
    fetched((got, got_sib), now_s, EDGE, HALF_NOW, 0, core)
    fetched((got, got_sib), old_s, 0, HALF_OLD, REST, core)
    receivers = [surface_at(lambda i: surf[i], n, n, STEPS) for n in range(2)]
    two_steps(now_r, old_r, med, new_r, edge.at[0], 1, receivers)
    shots = [shot_at(amount, spot, 0, n) for n in range(2)]
    two_steps(now_s, old_s, med, new_s, edge.at[1], 1, shots)
    for i in range(SPAN):
        at = SLAB * core + i
        carry[i] = new_r[at, EDGE : EDGE + rows, :]
        carry[SPAN + i] = new_s[at, EDGE : EDGE + rows, :]
        for k in range(3):
            carry[SPAN * (2 + k) + i] = med[k][at]
    for i in range(3):
        carry[SPAN * 5 + i] = surf[core + i]


def first_x(
    amount, spot, loc, sib, near, near_sib, got, got_sib, edge, carry,
    now, old, med_0, med_1, med_2, new,
):
    core, _ = position()
    refs = (loc, sib, near, near_sib)
    rows = loc.shape[1]
    med = (med_0, med_1, med_2)
    now_window(refs, now, SRC, core)
    rim_window(refs, old, SRC, core)
    for k in range(3):
        fetched((got, got_sib), med[k], 0, HALF_OLD, REST + HALF_OLD * (k + 1), core)
    two_steps(now, old, med, new, edge.at[0], 0, [shot_at(amount, spot, 1, n) for n in range(2)])
    for i in range(SPAN):
        at = SLAB * core + i
        carry[i] = new[at, EDGE : EDGE + rows, :]
        for k in range(3):
            carry[SPAN * (1 + k) + i] = med[k][at]


def halo_planes(last, edge, sides, window, pad):
    _, chip = position()
    for p in range(CHIP):
        place(window, CHIP + p, pad, edge[p])
        for src, side in sides:
            beyond = chip + 2 * side - 1
            plane = jnp.where((beyond >= 0) & (beyond <= last), src[p], 0.0)
            place(window, 2 * CHIP * side + p, pad, plane)


def product(first, second, slot, lags, b, pad, p, q):
    rows = first.shape[1] - 2 * pad
    lag = slot - (lags - 1) // 2
    if b + 8 <= abs(lag) or b >= rows - abs(lag):
        return None
    back, ahead = pad + b - lag, pad + b + lag
    return first[p, back : back + 8, :] * second[q, ahead : ahead + 8, :]


def middle(last, order, amount, spot, edge, near, carry, ahead, snap, slots, now_r, now_s):
    rows = carry.shape[1]
    pad = (now_r.shape[1] - rows) // 2
    core, _ = position()
    for n, now in enumerate((now_r, now_s)):
        clear(now, pad, rows)
        halo_planes(last, edge.at[n], ((near.at[n], core),), now, pad)
        term = shot_at(amount, spot, 0, 2)
        if n == 0:
            term = surface_at(lambda i: carry[SPAN * 5 + i], 0, 2, STEPS)
        advance(
            now, SLAB + CHIP * core, lambda i: carry[SPAN * n + i], SLAB * core,
            lambda k, i: carry[SPAN * (2 + k) + i], SLAB * core, ahead.at[n], 0,
            CHIP, pad, rows, 1, lambda i, b, size: term(i, b, size, SLAB * core),
        )
    hit = lax.broadcasted_iota(jnp.int32, (slots.shape[0], order.shape[1]), 0) == order[...]
    place_of = lax.broadcasted_iota(jnp.int32, hit.shape, 1).astype(jnp.float32)
    found = jnp.sum(jnp.where(hit, place_of, 0.0), axis=1, keepdims=True)
    slots[...] = jnp.broadcast_to(found, slots.shape)
    own = CHIP + SLAB * core
    for slot in range(snap.shape[0]):
        for p in range(SLAB):
            for b in range(0, rows, 8):
                value = product(now_s, now_r, slot, snap.shape[0], b, pad, own + p, own + p)
                if value is not None:
                    snap[slot, p, b : b + 8, :] = value


def last_steps(last, edges, n, now, old, med, new, end, across, extras, ahead=None):
    core, _ = position()
    edge, near, near_sib = edges
    rows = edge.shape[2]
    pad = (now.shape[1] - rows) // 2
    for window in (now, new, end):
        clear(window, pad, rows)
    halo_planes(last, edge.at[n], ((near.at[n], core), (near_sib.at[n], 1 - core)), now, pad)
    first, count = 0, SPAN
    if ahead is not None:
        for p in range(CHIP):
            place(new, SLAB * core + p, pad, ahead[n, p])
        first, count = CHIP * (1 - core), SLAB
    advance(
        now, SLAB * core + SLAB + first, old, first, med, first, new.at[pl.ds(first, count)], pad,
        count, pad, rows, across, lambda i, b, size: extras[0](i, b, size, first),
    )

    def older(i):
        return now[CHIP + SLAB * core + i, pad : pad + rows, :]

    advance(new, SLAB, older, 0, med, SLAB, end, pad, SLAB, pad, rows, across, extras[1])


def finish(end, new, following, prior, sems, at):
    rows = following.shape[1]
    inner = pl.ds((end.shape[1] - rows) // 2, rows)
    copies = [
        pltpu.make_async_copy(end.at[:, inner], following, sems.at[at]),
        pltpu.make_async_copy(new.at[pl.ds(SLAB, SLAB), inner], prior, sems.at[at + 1]),
    ]
    for copy in copies:
        copy.start()
    return copies


def second_half(
    last, amount, spot, edge, near, near_sib, carry, edge_x, near_x, sib_x, carry_x,
    ahead, snap, slots,
    src_next, src_prior, rcv_next, rcv_prior, image,
    now_r, now_s, now_x, new_r, new_s, new_x, end_r, end_s, end_x, planes, sems,
):
    rows, depth = carry.shape[1:]
    lags = image.shape[0]
    pad = (now_r.shape[1] - rows) // 2
    core, _ = position()
    def med(k, i):
        return carry[SPAN * (2 + k) + i]

    edges = (edge, near, near_sib)
    receivers = [surface_at(lambda i: carry[SPAN * 5 + i], n, 2 + n, STEPS) for n in range(2)]
    last_steps(last, edges, 0, now_r, lambda i: carry[i], med, new_r, end_r, 1, receivers, ahead)
    copies = finish(end_r, new_r, rcv_next, rcv_prior, sems, lags)
    shots = [shot_at(amount, spot, 0, 2 + n) for n in range(2)]
    last_steps(
        last, edges, 1, now_s, lambda i: carry[SPAN + i], med, new_s, end_s, 1, shots, ahead
    )
    shots = [shot_at(amount, spot, 1, 2 + n) for n in range(2)]
    last_steps(
        last, (edge_x, near_x, sib_x), 0, now_x, lambda i: carry_x[i],
        lambda k, i: carry_x[SPAN * (1 + k) + i], new_x, end_x, 0, shots,
    )
    copies += finish(end_x, new_x, src_next, src_prior, sems, lags + 2)
    for slot in range(lags):
        for p in range(SLAB):
            for b in range(0, rows, 8):
                value = product(end_s, end_r, slot, lags, b, pad, p, p)
                cut = slice(b, b + 8)
                if value is None:
                    planes[slot, p, cut, :] = jnp.zeros((8, depth), jnp.float32)
                else:
                    planes[slot, p, cut, :] = snap[slot, p, cut, :] + value
        copies.append(
            pltpu.make_async_copy(planes.at[slot], image.at[slots[slot, 0].astype(jnp.int32)], sems.at[slot])
        )
        copies[-1].start()
    for copy in copies:
        copy.wait()


def on_device(src_now, src_old, rcv_now, rcv_old, medium, wavelet, shot, traces, rec_x, lag_order):
    devices = lax.axis_size("wide")
    chips = devices // 2
    slab, rows, depth = src_now.shape
    assert slab == SLAB and rcv_now.shape == (SLAB, depth, rows) and wavelet.shape[0] == STEPS
    assert rows % 8 == 0 and rows == SLAB * devices
    lags = lag_order.shape[0]
    half = (lags - 1) // 2
    device = lax.axis_index("wide")
    chip, core = device // 2, device % 2
    last = chips - 1
    turning = chip == jnp.where(core == 0, last, 0)
    swap = [(i, i ^ 1) for i in range(devices)]
    order = [*range(0, devices, 2), *range(devices - 1, 0, -2)]
    ring = list(zip(order, order[1:] + order[:1]))

    def turned(x):
        return jnp.swapaxes(x, -1, -2)

    rcv_now, rcv_old, medium, traces = map(turned, (rcv_now, rcv_old, medium, traces))
    scalars = [pltpu.SMEM(shot.shape, jnp.int32), pltpu.SMEM(wavelet.shape, jnp.float32)]
    wide, loc, amount, spot = call(
        gather,
        (src_now, src_old, rcv_now, rcv_old, medium, traces, rec_x, shot, wavelet),
        [(5 * SLAB, rows + 2 * EDGE, depth), (7 * SLAB + 1, rows, depth)]
        + [(2, STEPS, 2 * CHIP, depth), (2, rows, depth)],
        [traces.shape],
        [pltpu.VMEM(rec_x.shape, jnp.int32), *scalars, pltpu.SemaphoreType.DMA((16,))],
        far=9,
    )
    (send,) = call(pack, (wide,), [(devices, SLAB * FETCH, depth)], [])
    got = lax.all_to_all(send, "wide", 0, 0, tiled=True).reshape(-1, depth)
    sib = lax.ppermute(loc, "wide", swap)
    low, high = jnp.where(core == 0, loc, sib), jnp.where(core == 0, sib, loc)
    rim = jnp.where(core == 0, high[2 * SLAB :], low[2 * SLAB :])
    ours = jnp.concatenate([low[: 2 * SLAB], high[: 2 * SLAB], rim])
    near = lax.ppermute(jnp.where(turning, 0.0, ours), "wide", ring)
    near_sib = lax.ppermute(near, "wide", swap)
    got_sib = lax.ppermute(got, "wide", swap)

    window, narrow = 3 * CHIP, 2 * CHIP
    padded, plain = (window, rows + 2 * EDGE, depth), (narrow, rows, depth)
    edge_y, carry_y = call(
        first_y,
        (amount, spot, loc, sib, near, near_sib, got, got_sib),
        [(2, CHIP, rows, depth), (SPAN * 5 + 3, rows, depth)],
        [padded] * 2 + [plain] * 5 + [(4, rows, depth)] + [(narrow, *padded[1:])] * 2,
    )
    mid_y = lax.ppermute(edge_y, "wide", ring)
    mid_y_sib = lax.ppermute(mid_y, "wide", swap)
    edge_x, carry_x = call(
        first_x,
        (amount, spot, loc, sib, near, near_sib, got, got_sib),
        [(1, CHIP, rows, depth), (SPAN * 4, rows, depth)],
        [padded] + [plain] * 4 + [(narrow, *padded[1:])],
    )
    mid_x = lax.ppermute(edge_x, "wide", ring)
    mid_x_sib = lax.ppermute(mid_x, "wide", swap)

    field = (SLAB, rows, depth)
    pad = -(-max(half, 2) // 8) * 8
    padded = (rows + 2 * pad, depth)
    ahead, snap, slots = call(
        functools.partial(middle, last),
        (lag_order[None], amount, spot, edge_y, mid_y, carry_y),
        [(2, CHIP, rows, depth), (lags, *field), (-(-lags // 8) * 8, depth)],
        [(window, *padded)] * 2,
    )
    src_next, src_prior, rcv_next, rcv_prior, image = call(
        functools.partial(second_half, last),
        (amount, spot, edge_y, mid_y, mid_y_sib, carry_y)
        + (edge_x, mid_x, mid_x_sib, carry_x, ahead, snap, slots),
        [field] * 4 + [(lags, *field)],
        [(window, *padded)] * 3 + [(SPAN, *padded)] * 3 + [(SLAB, *padded)] * 3 + [(lags, *field)],
        [pltpu.SemaphoreType.DMA((lags + 4,))],
        far_out=range(5),
    )
    return src_next, src_prior, turned(rcv_next), turned(rcv_prior), turned(image)


def solution(mesh):
    return jax.shard_map(
        on_device,
        mesh=mesh,
        in_specs=(
            P("wide", "shots", None),
            P("wide", "shots", None),
            P("wide", "shots", None),
            P("wide", "shots", None),
            P(None, "wide", None, None),
            P(),
            P("shots"),
            P("wide", "shots", None),
            P("wide", "shots"),
            P(),
        ),
        out_specs=(
            P("wide", "shots", None),
            P("wide", "shots", None),
            P("wide", "shots", None),
            P("wide", "shots", None),
            P("shots", "wide", None, None),
        ),
        check_vma=False,
    )
```

```python
import functools

import jax
import jax.numpy as jnp
from jax import lax
from jax.experimental import pallas as pl
from jax.experimental.pallas import tpu as pltpu
from jax.sharding import PartitionSpec as P

SLAB, CHIP, STEPS, EDGE = 2, 4, 4, 8
NEAR, FAR = 4.0 / 3.0, -1.0 / 12.0
RCV, SRC = 0, 1
SPAN = 3 * SLAB
HALF_NOW = (CHIP + 2 * CHIP) // 2
HALF_OLD = (CHIP + CHIP) // 2
FETCH = 24
REST = 8

VMEM = pl.BlockSpec(memory_space=pltpu.VMEM)
HBM = pl.BlockSpec(memory_space=pltpu.HBM)


def call(kernel, operands, outs, scratch, held=(), far=0, far_out=()):
    size = sum(4 * o.size for o in operands)
    size += sum(4 * functools.reduce(lambda a, b: a * b, s) for s in (*outs, *scratch))
    distant = [pltpu.with_memory_space_constraint(o, pltpu.HBM) for o in operands[:far]]
    return pl.pallas_call(
        kernel,
        out_shape=[jax.ShapeDtypeStruct(s, jnp.float32) for s in outs],
        in_specs=[HBM] * far + [VMEM] * (len(operands) - far),
        out_specs=[HBM if n in far_out else VMEM for n in range(len(outs))],
        scratch_shapes=[pltpu.VMEM(s, jnp.float32) for s in scratch] + list(held),
        compiler_params=pltpu.CompilerParams(vmem_limit_bytes=size + size // 4 + (8 << 20)),
    )(*distant, *operands[far:])


def position():
    device = lax.axis_index("wide")
    return lax.rem(device, 2), lax.div(device, 2)


def each(count, rows, body):
    if rows <= 32:
        for i in range(count):
            body(i)
    else:
        lax.fori_loop(0, count, lambda i, _: (body(i), 0)[1], 0)


def blocks(rows):
    size = min(rows, 32)
    return [(b, size) for b in range(0, rows, size)]


def gather(
    src_now, src_old, rcv_now, rcv_old, med, traces, rec_x, shot, wavelet,
    send, loc, amount, spot, wide, packed, traces_in, rec_in, shot_in, wavelet_in, sems,
):
    rows, depth = src_now.shape[1:]
    steps, cells = traces.shape[1], loc.shape[1]
    inner = pl.ds(EDGE, rows)
    pairs = []
    for n, own in enumerate((src_now, src_old, med.at[0], med.at[1], med.at[2])):
        pairs.append((own, wide.at[pl.ds(n * SLAB, SLAB), inner]))
    ready = len(pairs)
    pairs += [(traces, traces_in), (rec_x, rec_in), (shot, shot_in), (wavelet, wavelet_in)]
    for n, own in enumerate((rcv_now, src_now, rcv_old, src_old)):
        pairs.append((own, loc.at[pl.ds(n * SLAB, SLAB)]))
    pairs += [(med.at[k], loc.at[pl.ds((4 + k) * SLAB, SLAB)]) for k in range(3)]
    copies = [pltpu.make_async_copy(a, b, sems.at[n]) for n, (a, b) in enumerate(pairs)]
    for copy in copies:
        copy.start()
    clear(wide, EDGE, rows)
    for copy in copies[:ready]:
        copy.wait()
    pack(wide, packed)
    leaving = pltpu.make_async_copy(packed, send, sems.at[len(pairs)])
    leaving.start()
    for copy in copies[ready : ready + 4]:
        copy.wait()
    lane = lax.broadcasted_iota(jnp.int32, (cells, depth), 1)
    place = lax.broadcasted_iota(jnp.int32, (cells, rec_x.shape[1]), 0)
    surface = jnp.zeros((cells, depth), jnp.float32)
    for h in range(SLAB):
        hit = rec_in[h : h + 1, :] == place
        for s in range(steps):
            column = jnp.sum(jnp.where(hit, traces_in[h, s : s + 1, :], 0.0), axis=1, keepdims=True)
            surface = jnp.where(lane == steps * h + s, column, surface)
    loc[7 * SLAB] = surface
    core, chip = position()
    own = CHIP * chip + SLAB * core
    first = (CHIP * chip - SLAB, CHIP * chip, own - SLAB, own)
    plane = lax.broadcasted_iota(jnp.int32, amount.shape[2:], 0)
    row = lax.broadcasted_iota(jnp.int32, (cells, depth), 0)
    for chain, (at_plane, at_row) in enumerate(((1, 0), (0, 1))):
        here = (row == shot_in[at_row]) & (lane == shot_in[2])
        spot[chain] = jnp.where(here, 1.0, 0.0)
        for step in range(steps):
            hit = plane == shot_in[at_plane] - first[step]
            amount[chain, step] = jnp.where(hit, -wavelet_in[step], 0.0)
    for copy in copies[ready + 4 :]:
        copy.wait()
    leaving.wait()


def pack(wide, send):
    for j in range(send.shape[0]):
        chip, core = divmod(j, 2)
        now_at = EDGE + CHIP * chip - CHIP + HALF_NOW * core
        old_at = EDGE + CHIP * chip - SLAB + HALF_OLD * core
        for h in range(SLAB):
            at = FETCH * h
            send[j, at : at + HALF_NOW, :] = wide[h, now_at : now_at + HALF_NOW, :]
            for k in range(4):
                at = FETCH * h + REST + HALF_OLD * k
                plane = SLAB * (k + 1) + h
                send[j, at : at + HALF_OLD, :] = wide[plane, old_at : old_at + HALF_OLD, :]


def advance(now, now_at, old, old_at, med, med_at, new, new_pad, count, pad, rows, across, extra):
    depth = now.shape[2]
    lane = lax.broadcasted_iota(jnp.int32, (8, depth), 1)
    weight = [
        jnp.where(lane >= 1, NEAR, 0.0),
        jnp.where(lane < depth - 1, NEAR, 0.0),
        jnp.where(lane >= 2, FAR, 0.0),
        jnp.where(lane < depth - 2, FAR, 0.0),
    ]

    def one(i):
        w = now_at + i
        for b, size in blocks(rows):
            taps = [jnp.concatenate([t] * (size // 8), axis=0) for t in weight]

            def at(plane, shift):
                return now[plane, pad + b + shift : pad + b + shift + size, :]

            here = at(w, 0)
            centre = -2.5 * here
            plane_sum = (
                centre
                + NEAR * (at(w - 1, 0) + at(w + 1, 0))
                + FAR * (at(w - 2, 0) + at(w + 2, 0))
            )
            row_sum = (
                centre
                + NEAR * (at(w, -1) + at(w, 1))
                + FAR * (at(w, -2) + at(w, 2))
            )
            depth_sum = (
                centre
                + taps[0] * pltpu.roll(here, 1, 1)
                + taps[1] * pltpu.roll(here, depth - 1, 1)
                + taps[2] * pltpu.roll(here, 2, 1)
                + taps[3] * pltpu.roll(here, depth - 2, 1)
            )
            m = [med(k, med_at + i)[b : b + size, :] for k in range(3)]
            value = 2.0 * here - old(old_at + i)[b : b + size, :]
            value = value + m[across] * plane_sum + m[1 - across] * row_sum + m[2] * depth_sum
            if extra is not None:
                value = value + extra(i, b, size)
            new[i, new_pad + b : new_pad + b + size, :] = value

    each(count, rows, one)


def shot_at(amount, spot, chain, step):
    def extra(i, b, size, at=0):
        return amount[chain, step, pl.ds(at + i, 1), :] * spot[chain, b : b + size, :]

    return extra


def surface_at(surf, first, step, steps):
    def extra(i, b, size, at=0):
        held = surf(first + lax.div(at, SLAB) + i // SLAB)[b : b + size, :]
        depth = held.shape[1]
        lane = lax.broadcasted_iota(jnp.int32, (size, depth), 1)
        if isinstance(i, int):
            shift = (i % SLAB) * steps + step
            return jnp.where(lane == 0, pltpu.roll(held, (depth - shift) % depth, 1), 0.0)
        total = jnp.zeros_like(held)
        for s in range(SLAB):
            moved = pltpu.roll(held, (depth - s * steps - step) % depth, 1)
            total = jnp.where((lane == 0) & (i % SLAB == s), moved, total)
        return total

    return extra


def clear(window, pad, rows):
    count, _, depth = window.shape
    zero = jnp.zeros((count, pad, depth), jnp.float32)
    window[:, 0:pad, :] = zero
    window[:, pad + rows :, :] = zero


def place(window, at, pad, value):
    window[at, pad : pad + value.shape[0], :] = value


def own_planes(refs, window, pad, base, at, core):
    for src, q in ((refs[0], core), (refs[1], 1 - core)):
        for p in range(SLAB):
            place(window, base + SLAB * q + p, pad, src[at + p])


def side_planes(refs, window, pad, base, ats, core):
    for src, side in ((refs[0], core), (refs[1], 1 - core)):
        for n, at in enumerate(ats):
            for p in range(SLAB):
                place(window, base * side + SLAB * n + p, pad, src[at + p])


def now_window(refs, window, kind, core):
    own_planes(refs[:2], window, EDGE, CHIP, SLAB * kind, core)
    side_planes(refs[2:], window, EDGE, 2 * CHIP, (SLAB * kind, SLAB * (2 + kind)), core)


def rim_window(refs, window, kind, core):
    own_planes(refs[:2], window, 0, SLAB, SLAB * (2 + kind), core)
    side_planes(refs[2:], window, 0, SLAB + CHIP, (SLAB * (4 + kind),), core)


def two_steps(now, old, med, new, edge, across, extras):
    rows = edge.shape[1]
    count = old.shape[0]

    def medium(k, i):
        return med[k][i]

    clear(now, EDGE, rows)
    clear(new, EDGE, rows)
    advance(now, SLAB, lambda i: old[i], 0, medium, 0, new, EDGE, count, EDGE, rows, across, extras[0])
    advance(
        new, SLAB, lambda i: now[CHIP + i, EDGE : EDGE + rows, :], 0, medium, SLAB, edge, 0,
        CHIP, EDGE, rows, across, extras[1],
    )


def fetched(pair, window, pad, count, at, core):
    rows = window.shape[1] - 2 * pad
    for src, q in ((pair[0], core), (pair[1], 1 - core)):
        for p in range(count):
            place(window, count * q + p, pad, src[pl.ds(at + p, rows, stride=FETCH), :])


def first_y(
    amount, spot, loc, sib, near, near_sib, got, got_sib, edge, carry,
    now_r, now_s, old_r, old_s, med_0, med_1, med_2, surf, new_r, new_s,
):
    core, _ = position()
    refs = (loc, sib, near, near_sib)
    rows = loc.shape[1]
    med = (med_0, med_1, med_2)
    now_window(refs, now_r, RCV, core)
    rim_window(refs, old_r, RCV, core)
    for k in range(3):
        rim_window(refs, med[k], 2 + k, core)
    for n, ref in enumerate(refs):
        flip = core if n % 2 == 0 else 1 - core
        surf[1 + flip if n < 2 else 3 * flip] = ref[ref.shape[0] - 1]
    fetched((got, got_sib), now_s, EDGE, HALF_NOW, 0, core)
    fetched((got, got_sib), old_s, 0, HALF_OLD, REST, core)
    receivers = [surface_at(lambda i: surf[i], n, n, STEPS) for n in range(2)]
    two_steps(now_r, old_r, med, new_r, edge.at[0], 1, receivers)
    shots = [shot_at(amount, spot, 0, n) for n in range(2)]
    two_steps(now_s, old_s, med, new_s, edge.at[1], 1, shots)
    for i in range(SPAN):
        at = SLAB * core + i
        carry[i] = new_r[at, EDGE : EDGE + rows, :]
        carry[SPAN + i] = new_s[at, EDGE : EDGE + rows, :]
        for k in range(3):
            carry[SPAN * (2 + k) + i] = med[k][at]
    for i in range(3):
        carry[SPAN * 5 + i] = surf[core + i]


def first_x(
    amount, spot, loc, sib, near, near_sib, got, got_sib, edge, carry,
    now, old, med_0, med_1, med_2, new,
):
    core, _ = position()
    refs = (loc, sib, near, near_sib)
    rows = loc.shape[1]
    med = (med_0, med_1, med_2)
    now_window(refs, now, SRC, core)
    rim_window(refs, old, SRC, core)
    for k in range(3):
        fetched((got, got_sib), med[k], 0, HALF_OLD, REST + HALF_OLD * (k + 1), core)
    two_steps(now, old, med, new, edge.at[0], 0, [shot_at(amount, spot, 1, n) for n in range(2)])
    for i in range(SPAN):
        at = SLAB * core + i
        carry[i] = new[at, EDGE : EDGE + rows, :]
        for k in range(3):
            carry[SPAN * (1 + k) + i] = med[k][at]


def halo_planes(last, edge, sides, window, pad):
    _, chip = position()
    for p in range(CHIP):
        place(window, CHIP + p, pad, edge[p])
        for src, side in sides:
            beyond = chip + 2 * side - 1
            plane = jnp.where((beyond >= 0) & (beyond <= last), src[p], 0.0)
            place(window, 2 * CHIP * side + p, pad, plane)


def product(first, second, slot, lags, b, pad, p, q):
    rows = first.shape[1] - 2 * pad
    lag = slot - (lags - 1) // 2
    if b + 8 <= abs(lag) or b >= rows - abs(lag):
        return None
    back, ahead = pad + b - lag, pad + b + lag
    return first[p, back : back + 8, :] * second[q, ahead : ahead + 8, :]


def middle(last, order, amount, spot, edge, near, carry, ahead, snap, slots, now_r, now_s):
    rows = carry.shape[1]
    pad = (now_r.shape[1] - rows) // 2
    core, _ = position()
    for n, now in enumerate((now_r, now_s)):
        clear(now, pad, rows)
        halo_planes(last, edge.at[n], ((near.at[n], core),), now, pad)
        term = shot_at(amount, spot, 0, 2)
        if n == 0:
            term = surface_at(lambda i: carry[SPAN * 5 + i], 0, 2, STEPS)
        advance(
            now, SLAB + CHIP * core, lambda i: carry[SPAN * n + i], SLAB * core,
            lambda k, i: carry[SPAN * (2 + k) + i], SLAB * core, ahead.at[n], 0,
            CHIP, pad, rows, 1, lambda i, b, size: term(i, b, size, SLAB * core),
        )
    hit = lax.broadcasted_iota(jnp.int32, (slots.shape[0], order.shape[1]), 0) == order[...]
    place_of = lax.broadcasted_iota(jnp.int32, hit.shape, 1).astype(jnp.float32)
    found = jnp.sum(jnp.where(hit, place_of, 0.0), axis=1, keepdims=True)
    slots[...] = jnp.broadcast_to(found, slots.shape)
    own = CHIP + SLAB * core
    for slot in range(snap.shape[0]):
        for p in range(SLAB):
            for b in range(0, rows, 8):
                value = product(now_s, now_r, slot, snap.shape[0], b, pad, own + p, own + p)
                if value is not None:
                    snap[slot, p, b : b + 8, :] = value


def last_steps(last, edges, n, now, old, med, new, end, across, extras, ahead=None):
    core, _ = position()
    edge, near, near_sib = edges
    rows = edge.shape[2]
    pad = (now.shape[1] - rows) // 2
    for window in (now, new, end):
        clear(window, pad, rows)
    halo_planes(last, edge.at[n], ((near.at[n], core), (near_sib.at[n], 1 - core)), now, pad)
    first, count = 0, SPAN
    if ahead is not None:
        for p in range(CHIP):
            place(new, SLAB * core + p, pad, ahead[n, p])
        first, count = CHIP * (1 - core), SLAB
    advance(
        now, SLAB * core + SLAB + first, old, first, med, first, new.at[pl.ds(first, count)], pad,
        count, pad, rows, across, lambda i, b, size: extras[0](i, b, size, first),
    )

    def older(i):
        return now[CHIP + SLAB * core + i, pad : pad + rows, :]

    advance(new, SLAB, older, 0, med, SLAB, end, pad, SLAB, pad, rows, across, extras[1])


def finish(end, new, following, prior, sems, at):
    rows = following.shape[1]
    inner = pl.ds((end.shape[1] - rows) // 2, rows)
    copies = [
        pltpu.make_async_copy(end.at[:, inner], following, sems.at[at]),
        pltpu.make_async_copy(new.at[pl.ds(SLAB, SLAB), inner], prior, sems.at[at + 1]),
    ]
    for copy in copies:
        copy.start()
    return copies


def second_half(
    last, amount, spot, edge, near, near_sib, carry, edge_x, near_x, sib_x, carry_x,
    ahead, snap, slots,
    src_next, src_prior, rcv_next, rcv_prior, image,
    now_r, now_s, now_x, new_r, new_s, new_x, end_r, end_s, end_x, planes, sems,
):
    rows, depth = carry.shape[1:]
    lags = image.shape[0]
    pad = (now_r.shape[1] - rows) // 2
    core, _ = position()
    def med(k, i):
        return carry[SPAN * (2 + k) + i]

    edges = (edge, near, near_sib)
    receivers = [surface_at(lambda i: carry[SPAN * 5 + i], n, 2 + n, STEPS) for n in range(2)]
    last_steps(last, edges, 0, now_r, lambda i: carry[i], med, new_r, end_r, 1, receivers, ahead)
    copies = finish(end_r, new_r, rcv_next, rcv_prior, sems, lags)
    shots = [shot_at(amount, spot, 0, 2 + n) for n in range(2)]
    last_steps(
        last, edges, 1, now_s, lambda i: carry[SPAN + i], med, new_s, end_s, 1, shots, ahead
    )
    shots = [shot_at(amount, spot, 1, 2 + n) for n in range(2)]
    last_steps(
        last, (edge_x, near_x, sib_x), 0, now_x, lambda i: carry_x[i],
        lambda k, i: carry_x[SPAN * (1 + k) + i], new_x, end_x, 0, shots,
    )
    copies += finish(end_x, new_x, src_next, src_prior, sems, lags + 2)
    for slot in range(lags):
        for p in range(SLAB):
            for b in range(0, rows, 8):
                value = product(end_s, end_r, slot, lags, b, pad, p, p)
                cut = slice(b, b + 8)
                if value is None:
                    planes[slot, p, cut, :] = jnp.zeros((8, depth), jnp.float32)
                else:
                    planes[slot, p, cut, :] = snap[slot, p, cut, :] + value
        copies.append(
            pltpu.make_async_copy(planes.at[slot], image.at[slots[slot, 0].astype(jnp.int32)], sems.at[slot])
        )
        copies[-1].start()
    for copy in copies:
        copy.wait()


def on_device(src_now, src_old, rcv_now, rcv_old, medium, wavelet, shot, traces, rec_x, lag_order):
    devices = lax.axis_size("wide")
    chips = devices // 2
    slab, rows, depth = src_now.shape
    assert slab == SLAB and rcv_now.shape == (SLAB, depth, rows) and wavelet.shape[0] == STEPS
    assert rows % 8 == 0 and rows == SLAB * devices
    lags = lag_order.shape[0]
    half = (lags - 1) // 2
    device = lax.axis_index("wide")
    chip, core = device // 2, device % 2
    last = chips - 1
    turning = chip == jnp.where(core == 0, last, 0)
    swap = [(i, i ^ 1) for i in range(devices)]
    order = [*range(0, devices, 2), *range(devices - 1, 0, -2)]
    ring = list(zip(order, order[1:] + order[:1]))

    def turned(x):
        return jnp.swapaxes(x, -1, -2)

    rcv_now, rcv_old, medium, traces = map(turned, (rcv_now, rcv_old, medium, traces))
    scalars = [pltpu.SMEM(shot.shape, jnp.int32), pltpu.SMEM(wavelet.shape, jnp.float32)]
    send, loc, amount, spot = call(
        gather,
        (src_now, src_old, rcv_now, rcv_old, medium, traces, rec_x, shot, wavelet),
        [(devices, SLAB * FETCH, depth), (7 * SLAB + 1, rows, depth)]
        + [(2, STEPS, 2 * CHIP, depth), (2, rows, depth)],
        [(5 * SLAB, rows + 2 * EDGE, depth), (devices, SLAB * FETCH, depth), traces.shape],
        [pltpu.VMEM(rec_x.shape, jnp.int32), *scalars, pltpu.SemaphoreType.DMA((17,))],
        far=9,
        far_out=(0,),
    )
    got = lax.all_to_all(send, "wide", 0, 0, tiled=True).reshape(-1, depth)
    sib = lax.ppermute(loc, "wide", swap)
    low, high = jnp.where(core == 0, loc, sib), jnp.where(core == 0, sib, loc)
    rim = jnp.where(core == 0, high[2 * SLAB :], low[2 * SLAB :])
    ours = jnp.concatenate([low[: 2 * SLAB], high[: 2 * SLAB], rim])
    near = lax.ppermute(jnp.where(turning, 0.0, ours), "wide", ring)
    near_sib = lax.ppermute(near, "wide", swap)
    got_sib = lax.ppermute(got, "wide", swap)

    window, narrow = 3 * CHIP, 2 * CHIP
    padded, plain = (window, rows + 2 * EDGE, depth), (narrow, rows, depth)
    edge_y, carry_y = call(
        first_y,
        (amount, spot, loc, sib, near, near_sib, got, got_sib),
        [(2, CHIP, rows, depth), (SPAN * 5 + 3, rows, depth)],
        [padded] * 2 + [plain] * 5 + [(4, rows, depth)] + [(narrow, *padded[1:])] * 2,
    )
    mid_y = lax.ppermute(edge_y, "wide", ring)
    mid_y_sib = lax.ppermute(mid_y, "wide", swap)
    edge_x, carry_x = call(
        first_x,
        (amount, spot, loc, sib, near, near_sib, got, got_sib),
        [(1, CHIP, rows, depth), (SPAN * 4, rows, depth)],
        [padded] + [plain] * 4 + [(narrow, *padded[1:])],
    )
    mid_x = lax.ppermute(edge_x, "wide", ring)
    mid_x_sib = lax.ppermute(mid_x, "wide", swap)

    field = (SLAB, rows, depth)
    pad = -(-max(half, 2) // 8) * 8
    padded = (rows + 2 * pad, depth)
    ahead, snap, slots = call(
        functools.partial(middle, last),
        (lag_order[None], amount, spot, edge_y, mid_y, carry_y),
        [(2, CHIP, rows, depth), (lags, *field), (-(-lags // 8) * 8, depth)],
        [(window, *padded)] * 2,
    )
    src_next, src_prior, rcv_next, rcv_prior, image = call(
        functools.partial(second_half, last),
        (amount, spot, edge_y, mid_y, mid_y_sib, carry_y)
        + (edge_x, mid_x, mid_x_sib, carry_x, ahead, snap, slots),
        [field] * 4 + [(lags, *field)],
        [(window, *padded)] * 3 + [(SPAN, *padded)] * 3 + [(SLAB, *padded)] * 3 + [(lags, *field)],
        [pltpu.SemaphoreType.DMA((lags + 4,))],
        far_out=range(5),
    )
    return src_next, src_prior, turned(rcv_next), turned(rcv_prior), turned(image)


def solution(mesh):
    return jax.shard_map(
        on_device,
        mesh=mesh,
        in_specs=(
            P("wide", "shots", None),
            P("wide", "shots", None),
            P("wide", "shots", None),
            P("wide", "shots", None),
            P(None, "wide", None, None),
            P(),
            P("shots"),
            P("wide", "shots", None),
            P("wide", "shots"),
            P(),
        ),
        out_specs=(
            P("wide", "shots", None),
            P("wide", "shots", None),
            P("wide", "shots", None),
            P("wide", "shots", None),
            P("shots", "wide", None, None),
        ),
        check_vma=False,
    )
```

```python
import functools

import jax
import jax.numpy as jnp
from jax import lax
from jax.experimental import pallas as pl
from jax.experimental.pallas import tpu as pltpu
from jax.sharding import PartitionSpec as P

SLAB, CHIP, STEPS, EDGE = 2, 4, 4, 8
NEAR, FAR = 4.0 / 3.0, -1.0 / 12.0
RCV, SRC = 0, 1
SPAN = 3 * SLAB
HALF_NOW = (CHIP + 2 * CHIP) // 2
HALF_OLD = (CHIP + CHIP) // 2
FETCH = 24
REST = 8

VMEM = pl.BlockSpec(memory_space=pltpu.VMEM)
HBM = pl.BlockSpec(memory_space=pltpu.HBM)


def call(kernel, operands, outs, scratch, held=(), far=0, far_out=()):
    size = sum(4 * o.size for o in operands)
    size += sum(4 * functools.reduce(lambda a, b: a * b, s) for s in (*outs, *scratch))
    distant = [pltpu.with_memory_space_constraint(o, pltpu.HBM) for o in operands[:far]]
    return pl.pallas_call(
        kernel,
        out_shape=[jax.ShapeDtypeStruct(s, jnp.float32) for s in outs],
        in_specs=[HBM] * far + [VMEM] * (len(operands) - far),
        out_specs=[HBM if n in far_out else VMEM for n in range(len(outs))],
        scratch_shapes=[pltpu.VMEM(s, jnp.float32) for s in scratch] + list(held),
        compiler_params=pltpu.CompilerParams(vmem_limit_bytes=size + size // 4 + (8 << 20)),
    )(*distant, *operands[far:])


def position():
    device = lax.axis_index("wide")
    return lax.rem(device, 2), lax.div(device, 2)


def each(count, rows, body):
    if rows <= 32:
        for i in range(count):
            body(i)
    else:
        lax.fori_loop(0, count, lambda i, _: (body(i), 0)[1], 0)


def blocks(rows):
    size = min(rows, 32)
    return [(b, size) for b in range(0, rows, size)]


def gather(
    src_now, src_old, rcv_now, rcv_old, med, traces, rec_x, shot, wavelet,
    wide, loc, amount, spot, traces_in, rec_in, shot_in, wavelet_in, sems,
):
    rows, depth = src_now.shape[1:]
    steps, cells = traces.shape[1], loc.shape[1]
    inner = pl.ds(EDGE, rows)
    pairs = [(traces, traces_in), (rec_x, rec_in), (shot, shot_in), (wavelet, wavelet_in)]
    for n, own in enumerate((rcv_now, src_now, rcv_old, src_old)):
        pairs.append((own, loc.at[pl.ds(n * SLAB, SLAB)]))
    pairs += [(med.at[k], loc.at[pl.ds((4 + k) * SLAB, SLAB)]) for k in range(3)]
    for n, own in enumerate((src_now, src_old, med.at[0], med.at[1], med.at[2])):
        pairs.append((own, wide.at[pl.ds(n * SLAB, SLAB), inner]))
    copies = [pltpu.make_async_copy(a, b, sems.at[n]) for n, (a, b) in enumerate(pairs)]
    for copy in copies:
        copy.start()
    clear(wide, EDGE, rows)
    for copy in copies[:2]:
        copy.wait()
    lane = lax.broadcasted_iota(jnp.int32, (cells, depth), 1)
    place = lax.broadcasted_iota(jnp.int32, (cells, rec_x.shape[1]), 0)
    surface = jnp.zeros((cells, depth), jnp.float32)
    for h in range(SLAB):
        hit = rec_in[h : h + 1, :] == place
        for s in range(steps):
            column = jnp.sum(jnp.where(hit, traces_in[h, s : s + 1, :], 0.0), axis=1, keepdims=True)
            surface = jnp.where(lane == steps * h + s, column, surface)
    loc[7 * SLAB] = surface
    for copy in copies[2:4]:
        copy.wait()
    core, chip = position()
    own = CHIP * chip + SLAB * core
    first = (CHIP * chip - SLAB, CHIP * chip, own - SLAB, own)
    plane = lax.broadcasted_iota(jnp.int32, amount.shape[2:], 0)
    row = lax.broadcasted_iota(jnp.int32, (cells, depth), 0)
    for chain, (at_plane, at_row) in enumerate(((1, 0), (0, 1))):
        here = (row == shot_in[at_row]) & (lane == shot_in[2])
        spot[chain] = jnp.where(here, 1.0, 0.0)
        for step in range(steps):
            hit = plane == shot_in[at_plane] - first[step]
            amount[chain, step] = jnp.where(hit, -wavelet_in[step], 0.0)
    for copy in copies[4:]:
        copy.wait()


def pack(wide, send):
    for j in range(send.shape[0]):
        chip, core = divmod(j, 2)
        now_at = EDGE + CHIP * chip - CHIP + HALF_NOW * core
        old_at = EDGE + CHIP * chip - SLAB + HALF_OLD * core
        for h in range(SLAB):
            at = FETCH * h
            send[j, at : at + HALF_NOW, :] = wide[h, now_at : now_at + HALF_NOW, :]
            for k in range(4):
                at = FETCH * h + REST + HALF_OLD * k
                plane = SLAB * (k + 1) + h
                send[j, at : at + HALF_OLD, :] = wide[plane, old_at : old_at + HALF_OLD, :]


def advance(now, now_at, old, old_at, med, med_at, new, new_pad, count, pad, rows, across, extra):
    depth = now.shape[2]
    lane = lax.broadcasted_iota(jnp.int32, (8, depth), 1)
    weight = [
        jnp.where(lane >= 1, NEAR, 0.0),
        jnp.where(lane < depth - 1, NEAR, 0.0),
        jnp.where(lane >= 2, FAR, 0.0),
        jnp.where(lane < depth - 2, FAR, 0.0),
    ]

    def one(i):
        w = now_at + i
        for b, size in blocks(rows):
            taps = [jnp.concatenate([t] * (size // 8), axis=0) for t in weight]

            def at(plane, shift):
                return now[plane, pad + b + shift : pad + b + shift + size, :]

            here = at(w, 0)
            centre = -2.5 * here
            plane_sum = (
                centre
                + NEAR * (at(w - 1, 0) + at(w + 1, 0))
                + FAR * (at(w - 2, 0) + at(w + 2, 0))
            )
            row_sum = (
                centre
                + NEAR * (at(w, -1) + at(w, 1))
                + FAR * (at(w, -2) + at(w, 2))
            )
            depth_sum = (
                centre
                + taps[0] * pltpu.roll(here, 1, 1)
                + taps[1] * pltpu.roll(here, depth - 1, 1)
                + taps[2] * pltpu.roll(here, 2, 1)
                + taps[3] * pltpu.roll(here, depth - 2, 1)
            )
            m = [med(k, med_at + i)[b : b + size, :] for k in range(3)]
            value = 2.0 * here - old(old_at + i)[b : b + size, :]
            value = value + m[across] * plane_sum + m[1 - across] * row_sum + m[2] * depth_sum
            if extra is not None:
                value = value + extra(i, b, size)
            new[i, new_pad + b : new_pad + b + size, :] = value

    each(count, rows, one)


def shot_at(amount, spot, chain, step):
    def extra(i, b, size, at=0):
        return amount[chain, step, pl.ds(at + i, 1), :] * spot[chain, b : b + size, :]

    return extra


def surface_at(surf, first, step, steps):
    def extra(i, b, size, at=0):
        held = surf(first + lax.div(at, SLAB) + i // SLAB)[b : b + size, :]
        depth = held.shape[1]
        lane = lax.broadcasted_iota(jnp.int32, (size, depth), 1)
        if isinstance(i, int):
            shift = (i % SLAB) * steps + step
            return jnp.where(lane == 0, pltpu.roll(held, (depth - shift) % depth, 1), 0.0)
        total = jnp.zeros_like(held)
        for s in range(SLAB):
            moved = pltpu.roll(held, (depth - s * steps - step) % depth, 1)
            total = jnp.where((lane == 0) & (i % SLAB == s), moved, total)
        return total

    return extra


def clear(window, pad, rows):
    count, _, depth = window.shape
    zero = jnp.zeros((count, pad, depth), jnp.float32)
    window[:, 0:pad, :] = zero
    window[:, pad + rows :, :] = zero


def place(window, at, pad, value):
    window[at, pad : pad + value.shape[0], :] = value


def own_planes(refs, window, pad, base, at, core):
    for src, q in ((refs[0], core), (refs[1], 1 - core)):
        for p in range(SLAB):
            place(window, base + SLAB * q + p, pad, src[at + p])


def side_planes(refs, window, pad, base, ats, core):
    for src, side in ((refs[0], core), (refs[1], 1 - core)):
        for n, at in enumerate(ats):
            for p in range(SLAB):
                place(window, base * side + SLAB * n + p, pad, src[at + p])


def now_window(refs, window, kind, core):
    own_planes(refs[:2], window, EDGE, CHIP, SLAB * kind, core)
    side_planes(refs[2:], window, EDGE, 2 * CHIP, (SLAB * kind, SLAB * (2 + kind)), core)


def rim_window(refs, window, kind, core):
    own_planes(refs[:2], window, 0, SLAB, SLAB * (2 + kind), core)
    side_planes(refs[2:], window, 0, SLAB + CHIP, (SLAB * (4 + kind),), core)


def two_steps(now, old, med, new, edge, across, extras):
    rows = edge.shape[1]
    count = old.shape[0]

    def medium(k, i):
        return med[k][i]

    clear(now, EDGE, rows)
    clear(new, EDGE, rows)
    advance(now, SLAB, lambda i: old[i], 0, medium, 0, new, EDGE, count, EDGE, rows, across, extras[0])
    advance(
        new, SLAB, lambda i: now[CHIP + i, EDGE : EDGE + rows, :], 0, medium, SLAB, edge, 0,
        CHIP, EDGE, rows, across, extras[1],
    )


def fetched(pair, window, pad, count, at, core):
    rows = window.shape[1] - 2 * pad
    for src, q in ((pair[0], core), (pair[1], 1 - core)):
        for p in range(count):
            place(window, count * q + p, pad, src[pl.ds(at + p, rows, stride=FETCH), :])


def first_y(
    amount, spot, loc, sib, near, near_sib, got, got_sib, edge, carry,
    now_r, now_s, old_r, old_s, med_0, med_1, med_2, surf, new_r, new_s,
):
    core, _ = position()
    refs = (loc, sib, near, near_sib)
    rows = loc.shape[1]
    med = (med_0, med_1, med_2)
    now_window(refs, now_r, RCV, core)
    rim_window(refs, old_r, RCV, core)
    for k in range(3):
        rim_window(refs, med[k], 2 + k, core)
    for n, ref in enumerate(refs):
        flip = core if n % 2 == 0 else 1 - core
        surf[1 + flip if n < 2 else 3 * flip] = ref[ref.shape[0] - 1]
    fetched((got, got_sib), now_s, EDGE, HALF_NOW, 0, core)
    fetched((got, got_sib), old_s, 0, HALF_OLD, REST, core)
    receivers = [surface_at(lambda i: surf[i], n, n, STEPS) for n in range(2)]
    two_steps(now_r, old_r, med, new_r, edge.at[0], 1, receivers)
    shots = [shot_at(amount, spot, 0, n) for n in range(2)]
    two_steps(now_s, old_s, med, new_s, edge.at[1], 1, shots)
    for i in range(SPAN):
        at = SLAB * core + i
        carry[i] = new_r[at, EDGE : EDGE + rows, :]
        carry[SPAN + i] = new_s[at, EDGE : EDGE + rows, :]
        for k in range(3):
            carry[SPAN * (2 + k) + i] = med[k][at]
    for i in range(3):
        carry[SPAN * 5 + i] = surf[core + i]


def first_x(
    amount, spot, loc, sib, near, near_sib, got, got_sib, edge, carry,
    now, old, med_0, med_1, med_2, new,
):
    core, _ = position()
    refs = (loc, sib, near, near_sib)
    rows = loc.shape[1]
    med = (med_0, med_1, med_2)
    now_window(refs, now, SRC, core)
    rim_window(refs, old, SRC, core)
    for k in range(3):
        fetched((got, got_sib), med[k], 0, HALF_OLD, REST + HALF_OLD * (k + 1), core)
    two_steps(now, old, med, new, edge.at[0], 0, [shot_at(amount, spot, 1, n) for n in range(2)])
    for i in range(SPAN):
        at = SLAB * core + i
        carry[i] = new[at, EDGE : EDGE + rows, :]
        for k in range(3):
            carry[SPAN * (1 + k) + i] = med[k][at]


def halo_planes(last, edge, sides, window, pad):
    _, chip = position()
    for p in range(CHIP):
        place(window, CHIP + p, pad, edge[p])
        for src, side in sides:
            beyond = chip + 2 * side - 1
            plane = jnp.where((beyond >= 0) & (beyond <= last), src[p], 0.0)
            place(window, 2 * CHIP * side + p, pad, plane)


def product(first, second, slot, lags, b, pad, p, q):
    rows = first.shape[1] - 2 * pad
    lag = slot - (lags - 1) // 2
    if b + 8 <= abs(lag) or b >= rows - abs(lag):
        return None
    back, ahead = pad + b - lag, pad + b + lag
    return first[p, back : back + 8, :] * second[q, ahead : ahead + 8, :]


def middle(last, order, amount, spot, edge, near, carry, ahead, snap, slots, now_r, now_s):
    rows = carry.shape[1]
    pad = (now_r.shape[1] - rows) // 2
    core, _ = position()
    for n, now in enumerate((now_r, now_s)):
        clear(now, pad, rows)
        halo_planes(last, edge.at[n], ((near.at[n], core),), now, pad)
        term = shot_at(amount, spot, 0, 2)
        if n == 0:
            term = surface_at(lambda i: carry[SPAN * 5 + i], 0, 2, STEPS)
        advance(
            now, SLAB + CHIP * core, lambda i: carry[SPAN * n + i], SLAB * core,
            lambda k, i: carry[SPAN * (2 + k) + i], SLAB * core, ahead.at[n], 0,
            CHIP, pad, rows, 1, lambda i, b, size: term(i, b, size, SLAB * core),
        )
    hit = lax.broadcasted_iota(jnp.int32, (slots.shape[0], order.shape[1]), 0) == order[...]
    place_of = lax.broadcasted_iota(jnp.int32, hit.shape, 1).astype(jnp.float32)
    found = jnp.sum(jnp.where(hit, place_of, 0.0), axis=1, keepdims=True)
    slots[...] = jnp.broadcast_to(found, slots.shape)
    own = CHIP + SLAB * core
    for slot in range(snap.shape[0]):
        for p in range(SLAB):
            for b in range(0, rows, 8):
                value = product(now_s, now_r, slot, snap.shape[0], b, pad, own + p, own + p)
                if value is not None:
                    snap[slot, p, b : b + 8, :] = value


def last_steps(last, edges, n, now, old, med, new, end, across, extras, ahead=None):
    core, _ = position()
    edge, near, near_sib = edges
    rows = edge.shape[2]
    pad = (now.shape[1] - rows) // 2
    for window in (now, new, end):
        clear(window, pad, rows)
    halo_planes(last, edge.at[n], ((near.at[n], core), (near_sib.at[n], 1 - core)), now, pad)
    first, count = 0, SPAN
    if ahead is not None:
        for p in range(CHIP):
            place(new, SLAB * core + p, pad, ahead[n, p])
        first, count = CHIP * (1 - core), SLAB
    advance(
        now, SLAB * core + SLAB + first, old, first, med, first, new.at[pl.ds(first, count)], pad,
        count, pad, rows, across, lambda i, b, size: extras[0](i, b, size, first),
    )

    def older(i):
        return now[CHIP + SLAB * core + i, pad : pad + rows, :]

    advance(new, SLAB, older, 0, med, SLAB, end, pad, SLAB, pad, rows, across, extras[1])


def finish(end, new, following, prior, sems, at):
    rows = following.shape[1]
    inner = pl.ds((end.shape[1] - rows) // 2, rows)
    copies = [
        pltpu.make_async_copy(end.at[:, inner], following, sems.at[at]),
        pltpu.make_async_copy(new.at[pl.ds(SLAB, SLAB), inner], prior, sems.at[at + 1]),
    ]
    for copy in copies:
        copy.start()
    return copies


def second_half(
    last, amount, spot, edge, near, near_sib, carry, edge_x, near_x, sib_x, carry_x,
    ahead, snap, slots,
    src_next, src_prior, rcv_next, rcv_prior, image,
    now_r, now_s, now_x, new_r, new_s, new_x, end_r, end_s, end_x, planes, sems,
):
    rows, depth = carry.shape[1:]
    lags = image.shape[0]
    pad = (now_r.shape[1] - rows) // 2
    core, _ = position()
    def med(k, i):
        return carry[SPAN * (2 + k) + i]

    edges = (edge, near, near_sib)
    receivers = [surface_at(lambda i: carry[SPAN * 5 + i], n, 2 + n, STEPS) for n in range(2)]
    last_steps(last, edges, 0, now_r, lambda i: carry[i], med, new_r, end_r, 1, receivers, ahead)
    copies = finish(end_r, new_r, rcv_next, rcv_prior, sems, lags)
    shots = [shot_at(amount, spot, 0, 2 + n) for n in range(2)]
    last_steps(
        last, edges, 1, now_s, lambda i: carry[SPAN + i], med, new_s, end_s, 1, shots, ahead
    )
    for slot in range(lags):
        for p in range(SLAB):
            for b in range(0, rows, 8):
                value = product(end_s, end_r, slot, lags, b, pad, p, p)
                cut = slice(b, b + 8)
                if value is None:
                    planes[slot, p, cut, :] = jnp.zeros((8, depth), jnp.float32)
                else:
                    planes[slot, p, cut, :] = snap[slot, p, cut, :] + value
        copies.append(
            pltpu.make_async_copy(planes.at[slot], image.at[slots[slot, 0].astype(jnp.int32)], sems.at[slot])
        )
        copies[-1].start()
    shots = [shot_at(amount, spot, 1, 2 + n) for n in range(2)]
    last_steps(
        last, (edge_x, near_x, sib_x), 0, now_x, lambda i: carry_x[i],
        lambda k, i: carry_x[SPAN * (1 + k) + i], new_x, end_x, 0, shots,
    )
    copies += finish(end_x, new_x, src_next, src_prior, sems, lags + 2)
    for copy in copies:
        copy.wait()


def on_device(src_now, src_old, rcv_now, rcv_old, medium, wavelet, shot, traces, rec_x, lag_order):
    devices = lax.axis_size("wide")
    chips = devices // 2
    slab, rows, depth = src_now.shape
    assert slab == SLAB and rcv_now.shape == (SLAB, depth, rows) and wavelet.shape[0] == STEPS
    assert rows % 8 == 0 and rows == SLAB * devices
    lags = lag_order.shape[0]
    half = (lags - 1) // 2
    device = lax.axis_index("wide")
    chip, core = device // 2, device % 2
    last = chips - 1
    turning = chip == jnp.where(core == 0, last, 0)
    swap = [(i, i ^ 1) for i in range(devices)]
    order = [*range(0, devices, 2), *range(devices - 1, 0, -2)]
    ring = list(zip(order, order[1:] + order[:1]))

    def turned(x):
        return jnp.swapaxes(x, -1, -2)

    rcv_now, rcv_old, medium, traces = map(turned, (rcv_now, rcv_old, medium, traces))
    scalars = [pltpu.SMEM(shot.shape, jnp.int32), pltpu.SMEM(wavelet.shape, jnp.float32)]
    wide, loc, amount, spot = call(
        gather,
        (src_now, src_old, rcv_now, rcv_old, medium, traces, rec_x, shot, wavelet),
        [(5 * SLAB, rows + 2 * EDGE, depth), (7 * SLAB + 1, rows, depth)]
        + [(2, STEPS, 2 * CHIP, depth), (2, rows, depth)],
        [traces.shape],
        [pltpu.VMEM(rec_x.shape, jnp.int32), *scalars, pltpu.SemaphoreType.DMA((16,))],
        far=9,
    )
    (send,) = call(pack, (wide,), [(devices, SLAB * FETCH, depth)], [])
    got = lax.all_to_all(send, "wide", 0, 0, tiled=True).reshape(-1, depth)
    sib = lax.ppermute(loc, "wide", swap)
    low, high = jnp.where(core == 0, loc, sib), jnp.where(core == 0, sib, loc)
    rim = jnp.where(core == 0, high[2 * SLAB :], low[2 * SLAB :])
    ours = jnp.concatenate([low[: 2 * SLAB], high[: 2 * SLAB], rim])
    near = lax.ppermute(jnp.where(turning, 0.0, ours), "wide", ring)
    near_sib = lax.ppermute(near, "wide", swap)
    got_sib = lax.ppermute(got, "wide", swap)

    window, narrow = 3 * CHIP, 2 * CHIP
    padded, plain = (window, rows + 2 * EDGE, depth), (narrow, rows, depth)
    edge_y, carry_y = call(
        first_y,
        (amount, spot, loc, sib, near, near_sib, got, got_sib),
        [(2, CHIP, rows, depth), (SPAN * 5 + 3, rows, depth)],
        [padded] * 2 + [plain] * 5 + [(4, rows, depth)] + [(narrow, *padded[1:])] * 2,
    )
    mid_y = lax.ppermute(edge_y, "wide", ring)
    mid_y_sib = lax.ppermute(mid_y, "wide", swap)
    edge_x, carry_x = call(
        first_x,
        (amount, spot, loc, sib, near, near_sib, got, got_sib),
        [(1, CHIP, rows, depth), (SPAN * 4, rows, depth)],
        [padded] + [plain] * 4 + [(narrow, *padded[1:])],
    )
    mid_x = lax.ppermute(edge_x, "wide", ring)
    mid_x_sib = lax.ppermute(mid_x, "wide", swap)

    field = (SLAB, rows, depth)
    pad = -(-max(half, 2) // 8) * 8
    padded = (rows + 2 * pad, depth)
    ahead, snap, slots = call(
        functools.partial(middle, last),
        (lag_order[None], amount, spot, edge_y, mid_y, carry_y),
        [(2, CHIP, rows, depth), (lags, *field), (-(-lags // 8) * 8, depth)],
        [(window, *padded)] * 2,
    )
    src_next, src_prior, rcv_next, rcv_prior, image = call(
        functools.partial(second_half, last),
        (amount, spot, edge_y, mid_y, mid_y_sib, carry_y)
        + (edge_x, mid_x, mid_x_sib, carry_x, ahead, snap, slots),
        [field] * 4 + [(lags, *field)],
        [(window, *padded)] * 3 + [(SPAN, *padded)] * 3 + [(SLAB, *padded)] * 3 + [(lags, *field)],
        [pltpu.SemaphoreType.DMA((lags + 4,))],
        far_out=range(5),
    )
    return src_next, src_prior, turned(rcv_next), turned(rcv_prior), turned(image)


def solution(mesh):
    return jax.shard_map(
        on_device,
        mesh=mesh,
        in_specs=(
            P("wide", "shots", None),
            P("wide", "shots", None),
            P("wide", "shots", None),
            P("wide", "shots", None),
            P(None, "wide", None, None),
            P(),
            P("shots"),
            P("wide", "shots", None),
            P("wide", "shots"),
            P(),
        ),
        out_specs=(
            P("wide", "shots", None),
            P("wide", "shots", None),
            P("wide", "shots", None),
            P("wide", "shots", None),
            P("shots", "wide", None, None),
        ),
        check_vma=False,
    )
```
